128 devices in a mesh: tile: 32 (over x, z, core), rep: 4 (over y).
Axes of the slice: x: 4, y: 4, z: 4, core: 2. Of those that a mesh axis runs over, the one named last changes fastest.
Arguments:
- source: bfloat16 [32768, 256], P('tile'), may hold values from -20 to 20
- target: bfloat16 [32768, 256], P(('rep', 'tile')), may hold values from -20 to 20
- row_logw: float32 [32768], P('tile'), may hold values from -4 to 4
- col_logw: float32 [32768], P(('rep', 'tile')), may hold values from -4 to 4
- support: int32 [32, 32], replicated, may hold values from 0 to 1, as said below
Outputs:
- row_dual: float32 [32768], P('tile')
- col_dual: float32 [32768], P(('rep', 'tile'))
The draws below stay inside these ranges and needn't reach their ends.
Inputs may be any that keep to these rules, and one draw needn't show every extreme that they name: `support`: entries are 0 or 1; every row of blocks and every column of blocks holds at least one 1.
All inputs are finite; a program needn't handle non-finite values.
Results may differ from the reference program's by a relative error of at most 0.0004.
Values may be sent and summed in bfloat16 or wider, within the bound.
A program may use at most 128 MiB of HBM per device.

```python
import jax
import jax.numpy as jnp
from jax import lax

D = 256
ITERS = 2
NBLOCKS = 32
ROWS = 32768
COLS = 32768


def spread_cells(scale_key, values, top):
    count = values.shape[0]
    factors = jnp.exp(jnp.log(top) * jax.random.uniform(scale_key, (count, 1), jnp.float32))
    return (values * factors).astype(jnp.bfloat16)


def draw_source(key, part):
    key = jax.random.fold_in(key, 3)
    value_key, scale_key = jax.random.split(key)
    values = jax.random.truncated_normal(value_key, -4.0, 4.0, (ROWS, D), jnp.float32)
    return spread_cells(scale_key, values, 5.0)


def draw_target(key, part):
    key = jax.random.fold_in(key, 7)
    value_key, scale_key = jax.random.split(key)
    values = jax.random.truncated_normal(value_key, -4.0, 4.0, (COLS, D), jnp.float32)
    return spread_cells(scale_key, values, 5.0)


def draw_support(key, part):
    key = jax.random.fold_in(key, 11)
    first_key, second_key, third_key = jax.random.split(key, 3)
    levels = jax.random.randint(first_key, (NBLOCKS, 1), 100, 600)
    rolled = jax.random.randint(second_key, (NBLOCKS, NBLOCKS), 0, 1000)
    shuffled = jax.random.permutation(third_key, NBLOCKS)
    diagonal = shuffled[:, None] == jnp.arange(NBLOCKS)[None, :]
    return jnp.where((rolled < levels) | diagonal, 1, 0).astype(jnp.int32)


def level_of(own_key, shape, shards, smallest, largest):
    def one(dim, blocks):
        heights = jax.random.uniform(jax.random.fold_in(jax.random.fold_in(own_key, 6), dim), (blocks,), jnp.float32, smallest / len(shards), largest / len(shards))
        return jnp.repeat(jnp.exp(heights), shape[dim] // blocks).reshape((-1,) + (1,) * (len(shape) - dim - 1))

    level = one(*shards[0])
    for cut in shards[1:]:
        level = level * one(*cut)
    return level


def noise(key, shape, spread, limit, pieces=(), kind=jnp.bfloat16):
    values = spread * jax.random.normal(key, shape, jnp.float32)
    if pieces:
        values = values * level_of(key, shape, pieces, -0.22, 0.18)
    return jnp.clip(values, -limit, limit).astype(kind)


def setup_inputs(seed: int = 0) -> dict:
    seeds = jax.random.split(jax.random.key(seed), 6)
    return {
        "source": draw_source(jax.random.fold_in(seeds[5], 71), 0),
        "target": draw_target(jax.random.fold_in(seeds[5], 71), 0),
        "row_logw": noise(seeds[2], (ROWS,), 1.0, 4.0, ((0, 32),), jnp.float32),
        "col_logw": noise(seeds[3], (COLS,), 1.0, 4.0, ((0, 128),), jnp.float32),
        "support": draw_support(jax.random.fold_in(seeds[5], 71), 0),
    }


EPS = 0.1
NEG = -1.0e30


def merge_pairs(first, second):
    peak = jnp.maximum(first[0], second[0])
    return (peak, first[1] * jnp.exp(first[0] - peak) + second[1] * jnp.exp(second[0] - peak))


def reference(source, target, row_logw, col_logw, support):
    blocks = support.shape[0]
    block_rows = source.shape[0] // blocks
    width = source.shape[1]
    col_sq = jnp.sum(jnp.square(target.astype(jnp.float32)), axis=1)
    live_all = jnp.repeat(support > 0, block_rows, axis=1)
    grouped = source.reshape(blocks, block_rows, width)
    logs = row_logw.reshape(blocks, block_rows)

    def cost_for(rows):
        product = lax.dot_general(rows, target, (((1,), (1,)), ((), ())), preferred_element_type=jnp.float32)
        row_sq = jnp.sum(jnp.square(rows.astype(jnp.float32)), axis=1)
        return (row_sq[:, None] + col_sq[None, :] - 2.0 * product) / width

    potential = jnp.zeros((target.shape[0],), jnp.float32)
    duals = None
    for iteration in range(ITERS):
        def row_block(items):
            rows, live, weights = items
            cost = cost_for(rows)
            score = jnp.where(live[None, :], (potential[None, :] - cost) / EPS, NEG)
            peak = jnp.max(score, axis=1)
            total = jnp.sum(jnp.where(live[None, :], jnp.exp(score - peak[:, None]), 0.0), axis=1)
            return EPS * (weights - (peak + jnp.log(total)))

        duals = lax.map(row_block, (grouped, live_all, logs))

        def col_block(carry, items):
            rows, live, block_dual = items
            cost = cost_for(rows)
            score = jnp.where(live[None, :], (block_dual[:, None] - cost) / EPS, NEG)
            peak = jnp.max(score, axis=0)
            total = jnp.sum(jnp.where(live[None, :], jnp.exp(score - peak[None, :]), 0.0), axis=0)
            return merge_pairs(carry, (peak, total)), None

        start_vals = (jnp.full((target.shape[0],), NEG, jnp.float32), jnp.zeros((target.shape[0],), jnp.float32))
        (peak_all, total_all), unused = lax.scan(col_block, start_vals, (grouped, live_all, duals))
        potential = EPS * (col_logw - (peak_all + jnp.log(total_all)))
    return duals.reshape(-1), potential
```

```python
import functools
import math

import jax
import jax.numpy as jnp
from jax import lax
from jax.experimental import pallas as pl
from jax.experimental.pallas import tpu as pltpu
from jax.sharding import PartitionSpec as P

MESH = pl.DeviceIdType.MESH
ITERS = 2
EPS = 0.1
NEG = -1e30
LOG2E = 1.0 / math.log(2.0)
LN2 = math.log(2.0)
NX = 4
TILES = 2 * NX * NX
REPS = 4
LANES = 128


def kernel(
    source_hbm,
    target_hbm,
    row_logw,
    col_logw,
    support,
    row_out,
    col_out,
    src,
    tgt,
    prod,
    m_run,
    s_run,
    b_col,
    a_all,
    a_wide,
    row_part,
    col_part,
    col_in,
    local_sem,
    gather_send,
    gather_recv,
    a_send,
    a_recv,
    row_send,
    row_recv,
    col_send,
    col_recv,
):
    rows = src.shape[0]
    shard = tgt.shape[1]
    depth = src.shape[1]
    blocks = TILES * shard // rows
    per_block = TILES // blocks
    chunks = rows // LANES
    me = lax.axis_index("tile")
    rep = lax.axis_index("rep")
    core = me % 2
    x = me // (2 * NX)
    z = (me // 2) % NX
    first = x * (1 - core) + z * core
    second = z * (1 - core) + x * core
    score_scale = 2.0 * LOG2E / (depth * EPS)
    square_scale = LOG2E / (depth * EPS)
    dual_scale = EPS * LN2

    def tile_of(core_id, da, db):
        a = (first + da + NX) % NX
        b = (second + db + NX) % NX
        return ((a * NX + b) * (1 - core_id) + (b * NX + a) * core_id) * 2 + core_id

    def mine(da, db):
        return tile_of(core, da, db)

    partner = me + 1 - 2 * core

    def partners(da, db):
        a = (second + da + NX) % NX
        b = (first + db + NX) % NX
        other = 1 - core
        return ((a * NX + b) * (1 - other) + (b * NX + a) * other) * 2 + other

    barrier = pltpu.get_barrier_semaphore()

    def greet(step, carry):
        to = (me + step) % TILES
        pl.semaphore_signal(barrier, inc=1, device_id={"tile": to}, device_id_type=MESH)
        return carry

    load_src = pltpu.make_async_copy(source_hbm, src, local_sem.at[0])
    load_src.start()
    load_tgt = pltpu.make_async_copy(target_hbm, tgt.at[me], local_sem.at[1])
    load_tgt.start()
    lax.fori_loop(1, TILES, greet, 0)
    for step in range(1, REPS):
        to = (rep + step) % REPS
        pl.semaphore_signal(barrier, inc=1, device_id={"rep": to}, device_id_type=MESH)
    pl.semaphore_wait(barrier, TILES - 1 + REPS - 1)

    half = shard // 2

    def send_shard(k, to, part=None, source=None):
        if part is None:
            view, sem = tgt.at[k], gather_recv.at[0, k]
        else:
            view, sem = tgt.at[k, pl.ds(part * half, half)], gather_recv.at[part, k]
        pltpu.make_async_remote_copy(
            src_ref=view if source is None else source,
            dst_ref=view,
            send_sem=gather_send.at[0],
            recv_sem=sem,
            device_id={"tile": to},
            device_id_type=MESH,
        ).start()

    def wait_shard(k, parts):
        if parts == 1:
            pltpu.make_async_copy(tgt.at[k], tgt.at[k], gather_recv.at[0, k]).wait()
        else:
            for part in range(2):
                view = tgt.at[k, pl.ds(part * half, half)]
                pltpu.make_async_copy(view, view, gather_recv.at[part, k]).wait()

    send_shard(me, mine(1, 0), source=target_hbm)
    send_shard(me, mine(-1, 0), source=target_hbm)
    send_shard(me, mine(0, 1), source=target_hbm)
    send_shard(me, mine(0, -1), source=target_hbm)
    send_shard(me, partner, source=target_hbm)

    def send_potential(iteration):
        def one(step, carry):
            to = (me + step) % TILES
            pltpu.make_async_remote_copy(
                src_ref=a_all.at[iteration, me],
                dst_ref=a_all.at[iteration, me],
                send_sem=a_send.at[iteration],
                recv_sem=a_recv.at[iteration],
                device_id={"tile": to},
                device_id_type=MESH,
            ).start()
            return carry

        lax.fori_loop(1, TILES, one, 0)

    def wait_potential(iteration):
        view = a_all.at[iteration, pl.ds(0, TILES - 1)]
        pltpu.make_async_copy(view, view, a_recv.at[iteration]).wait()

    def bias_of(k):
        live = support[me, rep * blocks + k // per_block]
        return (1.0 - live.astype(jnp.float32)) * NEG

    load_tgt.wait()
    own = tgt[me].astype(jnp.float32)
    own_sq = jnp.sum((own * own).T, axis=0, keepdims=True)
    a_all[0, me] = -square_scale * own_sq
    send_potential(0)

    m_run[...] = jnp.full(m_run.shape, NEG, jnp.float32)
    s_run[...] = jnp.zeros(s_run.shape, jnp.float32)
    load_src.wait()

    row_block = min(512, rows)

    def first_rows(k):
        a = a_all[0, k] + bias_of(k)
        cells = tgt[k]

        def some(step, carry):
            at = pl.ds(pl.multiple_of(step * row_block, row_block), row_block)
            p = score_scale * lax.dot_general(
                src[at, :], cells, (((1,), (1,)), ((), ())), preferred_element_type=jnp.float32
            )
            prod[k, at, :] = p
            old = m_run[at, :]
            t = [
                p[:, i * LANES : (i + 1) * LANES] + a[:, i * LANES : (i + 1) * LANES]
                for i in range(shard // LANES)
            ]
            new = functools.reduce(jnp.maximum, t, old)
            m_run[at, :] = new
            s_run[at, :] = s_run[at, :] * jnp.exp2(old - new) + sum(jnp.exp2(v - new) for v in t)
            return carry

        lax.fori_loop(0, rows // row_block, some, 0)

    k = mine(-1, 0)
    wait_shard(k, 1)
    for to in (mine(0, 1), mine(0, -1)):
        send_shard(k, to)
    send_shard(k, mine(1, 0), part=0)
    send_shard(k, partner)
    k = mine(1, 0)
    wait_shard(k, 1)
    for to in (mine(0, 1), mine(0, -1)):
        send_shard(k, to)
    send_shard(k, mine(-1, 0), part=1)
    send_shard(k, partner)
    wait_potential(0)
    first_rows(me)

    def pass_along_second(da):
        k = mine(da, -1)
        wait_shard(k, 1)
        send_shard(k, mine(0, 1), part=0)
        send_shard(k, partner)
        k = mine(da, 1)
        wait_shard(k, 1)
        send_shard(k, mine(0, -1), part=1)
        send_shard(k, partner)

    k = mine(2, 0)
    wait_shard(k, 2)
    for to in (mine(0, 1), mine(0, -1)):
        send_shard(k, to)
    send_shard(k, partner)
    pass_along_second(0)
    k = partner
    wait_shard(k, 1)
    first_rows(k)
    first_rows(mine(-1, 0))
    first_rows(mine(1, 0))
    pass_along_second(-1)
    first_rows(mine(2, 0))
    first_rows(mine(0, -1))
    first_rows(mine(0, 1))
    pass_along_second(1)
    for da, db in ((-1, 0), (1, 0), (2, 0), (0, -1), (0, 1)):
        k = partners(da, db)
        wait_shard(k, 1)
        first_rows(k)
    pass_along_second(2)
    for da in (-1, 1, 2):
        first_rows(mine(da, -1))
        first_rows(mine(da, 1))
    for da in (0, -1, 1, 2):
        k = mine(da, 2)
        wait_shard(k, 2)
        send_shard(k, partner)
    for da in (-1, 1, 2):
        for db in (-1, 1):
            k = partners(da, db)
            wait_shard(k, 1)
            first_rows(k)
    for da in (0, -1, 1, 2):
        first_rows(mine(da, 2))
    for da in (0, -1, 1, 2):
        k = partners(da, 2)
        wait_shard(k, 1)
        first_rows(k)

    def send_view(parts):
        return tgt.at[pl.ds(0, parts)]

    def finish_rows(iteration):
        def fold(q, carry):
            at = pl.ds(pl.multiple_of(q * LANES, LANES), LANES)
            m = m_run[at, :].T
            s = s_run[at, :].T
            peak = jnp.max(m, axis=0, keepdims=True)
            total = jnp.sum(s * jnp.exp2(m - peak), axis=0, keepdims=True)
            row_part[iteration, rep, pl.ds(q, 1), :] = peak + jnp.log2(total)
            return carry

        lax.fori_loop(0, chunks, fold, 0)
        for step in range(1, REPS):
            to = (rep + step) % REPS
            pltpu.make_async_remote_copy(
                src_ref=row_part.at[iteration, rep],
                dst_ref=row_part.at[iteration, rep],
                send_sem=row_send.at[iteration],
                recv_sem=row_recv.at[iteration],
                device_id={"rep": to},
                device_id_type=MESH,
            ).start()
        view = row_part.at[iteration, pl.ds(0, REPS - 1)]
        pltpu.make_async_copy(view, view, row_recv.at[iteration]).wait()
        parts = [row_part[iteration, i] for i in range(REPS)]
        peak = functools.reduce(jnp.maximum, parts)
        total = sum(jnp.exp2(v - peak) for v in parts)
        b = LOG2E * row_logw[...] - (peak + jnp.log2(total))
        for q in range(chunks):
            b_col[q * LANES : (q + 1) * LANES, :] = jnp.broadcast_to(
                b[q : q + 1, :], (LANES, LANES)
            ).T
        return b

    groups = LANES // 8

    def columns_of(k, iteration):
        bias = bias_of(k)
        for i in range(shard // LANES):
            lanes = slice(i * LANES, (i + 1) * LANES)
            peak = jnp.full((8, LANES), NEG, jnp.float32)
            total = jnp.zeros((8, LANES), jnp.float32)
            for q in range(chunks):
                at = slice(q * LANES, (q + 1) * LANES)
                t = (prod[k, at, lanes] + b_col[at, :]).reshape(groups, 8, LANES)
                new = jnp.maximum(peak, jnp.max(t, axis=0))
                total = total * jnp.exp2(peak - new) + jnp.sum(jnp.exp2(t - new[None]), axis=0)
                peak = new
            top = jnp.max(peak, axis=0, keepdims=True)
            total = jnp.sum(total * jnp.exp2(peak - top), axis=0, keepdims=True)
            col_part[iteration, k, :, lanes] = top + jnp.log2(total) + bias

    def column_pass(iteration):
        def one(step, carry):
            k = (me + step) % TILES
            columns_of(k, iteration)
            pltpu.make_async_remote_copy(
                src_ref=col_part.at[iteration, k],
                dst_ref=col_in.at[iteration, step - 1],
                send_sem=col_send.at[iteration],
                recv_sem=col_recv.at[iteration],
                device_id={"tile": k},
                device_id_type=MESH,
            ).start()
            return carry

        lax.fori_loop(1, TILES, one, 0)
        columns_of(me, iteration)
        col_in[iteration, TILES - 1] = col_part[iteration, me]
        view = col_in.at[iteration, pl.ds(0, TILES - 1)]
        pltpu.make_async_copy(view, view, col_recv.at[iteration]).wait()
        parts = col_in[iteration]
        peak = jnp.max(parts, axis=0)
        total = jnp.sum(jnp.exp2(parts - peak[None]), axis=0)
        return LOG2E * col_logw[...] - (peak + jnp.log2(total))

    step_rows = 16
    wide = 8

    def row_pass(iteration):
        def spread(k, carry):
            a = a_all[iteration, k] + bias_of(k)
            a_wide[k] = jnp.broadcast_to(a, (8, shard))
            return carry

        lax.fori_loop(0, TILES, spread, 0)

        def some(step, carry):
            at = pl.ds(pl.multiple_of(step * step_rows, step_rows), step_rows)
            peak = jnp.full((step_rows // 8, 8, LANES), NEG, jnp.float32)
            total = jnp.zeros((step_rows // 8, 8, LANES), jnp.float32)
            for k0 in range(0, TILES, wide):
                t = []
                for k in range(k0, k0 + wide):
                    p = prod[k, at, :].reshape(step_rows // 8, 8, shard) + a_wide[k][None]
                    t.extend(p[:, :, i * LANES : (i + 1) * LANES] for i in range(shard // LANES))
                new = functools.reduce(jnp.maximum, t, peak)
                total = total * jnp.exp2(peak - new) + sum(jnp.exp2(v - new) for v in t)
                peak = new
            m_run[at, :] = peak.reshape(step_rows, LANES)
            s_run[at, :] = total.reshape(step_rows, LANES)
            return carry

        lax.fori_loop(0, rows // step_rows, some, 0)

    b = finish_rows(0)
    a = column_pass(0)
    for iteration in range(1, ITERS):
        a_all[iteration, me] = a
        send_potential(iteration)
        wait_potential(iteration)
        row_pass(iteration)
        b = finish_rows(iteration)
        a = column_pass(iteration)

    for q in range(chunks):
        cells = src[q * LANES : (q + 1) * LANES, :].astype(jnp.float32)
        sq = cells * cells
        sq = sum(sq[:, i * LANES : (i + 1) * LANES] for i in range(depth // LANES))
        row_out[q : q + 1, :] = jnp.sum(sq.T, axis=0, keepdims=True) / depth
    row_out[...] = row_out[...] + dual_scale * b
    col_out[...] = own_sq / depth + dual_scale * a

    view = send_view(TILES - 1)
    pltpu.make_async_copy(view, view, gather_send.at[0]).wait()
    for iteration in range(ITERS):
        view = a_all.at[iteration, pl.ds(0, TILES - 1)]
        pltpu.make_async_copy(view, view, a_send.at[iteration]).wait()
        view = row_part.at[iteration, pl.ds(0, REPS - 1)]
        pltpu.make_async_copy(view, view, row_send.at[iteration]).wait()
        view = col_part.at[iteration, pl.ds(0, TILES - 1)]
        pltpu.make_async_copy(view, view, col_send.at[iteration]).wait()


def per_device(source, target, row_logw, col_logw, support):
    rows, depth = source.shape
    shard = target.shape[0]
    vmem = pl.BlockSpec(memory_space=pltpu.VMEM)
    row_dual, col_dual = pl.pallas_call(
        kernel,
        out_shape=(
            jax.ShapeDtypeStruct((rows // LANES, LANES), jnp.float32),
            jax.ShapeDtypeStruct((1, shard), jnp.float32),
        ),
        in_specs=[
            pl.BlockSpec(memory_space=pl.ANY),
            pl.BlockSpec(memory_space=pl.ANY),
            vmem,
            vmem,
            pl.BlockSpec(memory_space=pltpu.SMEM),
        ],
        out_specs=(vmem, vmem),
        scratch_shapes=[
            pltpu.VMEM((rows, depth), source.dtype),
            pltpu.VMEM((TILES, shard, depth), target.dtype),
            pltpu.VMEM((TILES, rows, shard), jnp.float32),
            pltpu.VMEM((rows, LANES), jnp.float32),
            pltpu.VMEM((rows, LANES), jnp.float32),
            pltpu.VMEM((rows, LANES), jnp.float32),
            pltpu.VMEM((ITERS, TILES, 1, shard), jnp.float32),
            pltpu.VMEM((TILES, 8, shard), jnp.float32),
            pltpu.VMEM((ITERS, REPS, rows // LANES, LANES), jnp.float32),
            pltpu.VMEM((ITERS, TILES, 1, shard), jnp.float32),
            pltpu.VMEM((ITERS, TILES, 1, shard), jnp.float32),
            pltpu.SemaphoreType.DMA((2,)),
            pltpu.SemaphoreType.DMA((1,)),
            pltpu.SemaphoreType.DMA((2, TILES)),
            pltpu.SemaphoreType.DMA((ITERS,)),
            pltpu.SemaphoreType.DMA((ITERS,)),
            pltpu.SemaphoreType.DMA((ITERS,)),
            pltpu.SemaphoreType.DMA((ITERS,)),
            pltpu.SemaphoreType.DMA((ITERS,)),
            pltpu.SemaphoreType.DMA((ITERS,)),
        ],
        compiler_params=pltpu.CompilerParams(
            collective_id=0, has_side_effects=True, vmem_limit_bytes=52 * 1024 * 1024
        ),
        name="sinkhorn",
    )(
        source,
        target,
        row_logw.reshape(rows // LANES, LANES),
        col_logw.reshape(1, shard),
        support,
    )
    return row_dual.reshape(rows), col_dual.reshape(shard)


def solution(mesh):
    placed = (P("tile", None), P(("rep", "tile"), None), P("tile"), P(("rep", "tile")), P())
    return jax.shard_map(
        per_device,
        mesh=mesh,
        in_specs=placed,
        out_specs=(P("tile"), P(("rep", "tile"))),
        check_vma=False,
    )
```

```python
import functools
import math

import jax
import jax.numpy as jnp
from jax import lax
from jax.experimental import pallas as pl
from jax.experimental.pallas import tpu as pltpu
from jax.sharding import PartitionSpec as P

MESH = pl.DeviceIdType.MESH
EPS = 0.1
NEG = -1e30
LOG2E = 1.0 / math.log(2.0)
LN2 = math.log(2.0)
NX = 4
TILES = 2 * NX * NX
REPS = 4
LANES = 128


def kernel(
    source_hbm,
    target_hbm,
    row_logw_hbm,
    col_logw_hbm,
    support_hbm,
    row_out,
    col_out,
    src,
    tgt,
    row_logw,
    col_logw,
    support,
    prod,
    stage_a,
    stage_b,
    m_run,
    s_run,
    b_col,
    a_all,
    a_wide,
    row_sq,
    row_part,
    col_part,
    col_in,
    local_sem,
    gather_send,
    gather_recv,
    a_send,
    a_recv,
    row_send,
    row_recv,
    col_send,
    col_recv,
):
    rows = src.shape[0]
    shard = tgt.shape[1]
    depth = src.shape[1]
    blocks = TILES * shard // rows
    per_block = TILES // blocks
    chunks = rows // LANES
    halves = shard // LANES
    me = lax.axis_index("tile")
    rep = lax.axis_index("rep")
    core = me % 2
    x = me // (2 * NX)
    z = (me // 2) % NX
    first = x * (1 - core) + z * core
    second = z * (1 - core) + x * core
    score_scale = 2.0 * LOG2E / (depth * EPS)
    square_scale = LOG2E / (depth * EPS)
    dual_scale = EPS * LN2

    def mine(da, db):
        a = (first + da) % NX
        b = (second + db) % NX
        return ((a * NX + b) * (1 - core) + (b * NX + a) * core) * 2 + core

    def theirs(da, db):
        a = (second + da) % NX
        b = (first + db) % NX
        return ((a * NX + b) * core + (b * NX + a) * (1 - core)) * 2 + 1 - core

    partner = me + 1 - 2 * core

    def far_first(n):
        m = NX - 1 - n
        return m + m // 2 - 2 * (m // 3)

    def peer(step):
        dx = far_first(step // 8)
        dz = far_first((step // 2) % 4)
        dc = 1 - step % 2
        return (((x + dx) % NX) * NX + (z + dz) % NX) * 2 + (core + dc) % 2

    loads = [
        pltpu.make_async_copy(target_hbm, tgt.at[me], local_sem.at[0]),
        pltpu.make_async_copy(source_hbm, src, local_sem.at[1]),
        pltpu.make_async_copy(support_hbm, support, local_sem.at[2]),
        pltpu.make_async_copy(row_logw_hbm, row_logw, local_sem.at[3]),
        pltpu.make_async_copy(col_logw_hbm, col_logw, local_sem.at[4]),
    ]
    for load in loads:
        load.start()

    barrier = pltpu.get_barrier_semaphore()

    def greet(step, carry):
        pl.semaphore_signal(
            barrier, inc=1, device_id={"tile": peer(step)}, device_id_type=MESH
        )
        return carry

    lax.fori_loop(0, TILES - 1, greet, 0)
    for step in range(1, REPS):
        to = (rep + step) % REPS
        pl.semaphore_signal(barrier, inc=1, device_id={"rep": to}, device_id_type=MESH)
    pl.semaphore_wait(barrier, TILES - 1 + REPS - 1)

    def send_shard(k, to, source=None):
        view = tgt.at[k]
        pltpu.make_async_remote_copy(
            src_ref=view if source is None else source,
            dst_ref=view,
            send_sem=gather_send.at[0],
            recv_sem=gather_recv.at[k],
            device_id={"tile": to},
            device_id_type=MESH,
        ).start()

    def wait_shard(k):
        pltpu.make_async_copy(tgt.at[k], tgt.at[k], gather_recv.at[k]).wait()

    for step in (1, 3, 2):
        send_shard(me, mine(step, 0), source=target_hbm)
    send_shard(me, partner, source=target_hbm)
    for step in (1, 3, 2):
        send_shard(me, mine(0, step), source=target_hbm)

    def send_potential(iteration):
        def one(step, carry):
            pltpu.make_async_remote_copy(
                src_ref=a_all.at[iteration, me],
                dst_ref=a_all.at[iteration, me],
                send_sem=a_send.at[iteration],
                recv_sem=a_recv.at[iteration],
                device_id={"tile": peer(step)},
                device_id_type=MESH,
            ).start()
            return carry

        lax.fori_loop(0, TILES - 1, one, 0)

    def wait_potential(iteration):
        view = a_all.at[iteration, pl.ds(0, TILES - 1)]
        pltpu.make_async_copy(view, view, a_recv.at[iteration]).wait()

    def bias_of(k):
        live = support[me, rep * blocks + k // per_block]
        return (1.0 - live.astype(jnp.float32)) * NEG

    loads[0].wait()
    own = tgt[me].astype(jnp.float32)
    own_sq = jnp.sum((own * own).T, axis=0, keepdims=True)
    a_all[0, me] = -square_scale * own_sq
    send_potential(0)
    for load in loads[1:]:
        load.wait()

    m_run[...] = jnp.full(m_run.shape, NEG, jnp.float32)
    s_run[...] = jnp.zeros(s_run.shape, jnp.float32)
    for q in range(chunks):
        cells = src[q * LANES : (q + 1) * LANES, :].astype(jnp.float32)
        sq = cells * cells
        sq = sum(sq[:, i * LANES : (i + 1) * LANES] for i in range(depth // LANES))
        row_sq[q : q + 1, :] = jnp.sum(sq.T, axis=0, keepdims=True)

    tall = 512

    def products(pair, stage):
        for i, k in enumerate(pair):
            cells = tgt[k]
            for r in range(0, rows, tall):
                stage[i, r : r + tall, :] = lax.dot_general(
                    src[r : r + tall, :],
                    cells,
                    (((1,), (1,)), ((), ())),
                    preferred_element_type=jnp.float32,
                )

    def update(pair, stage):
        terms = [a_all[0, k] + bias_of(k) for k in pair]
        step = 32
        for r in range(0, rows, step):
            at = slice(r, r + step)
            t = []
            for i, k in enumerate(pair):
                p = stage[i, at, :] * score_scale
                prod[k, at, :] = p
                t.extend(
                    p[:, h * LANES : (h + 1) * LANES] + terms[i][:, h * LANES : (h + 1) * LANES]
                    for h in range(halves)
                )
            old = m_run[at, :]
            new = functools.reduce(jnp.maximum, t, old)
            m_run[at, :] = new
            s_run[at, :] = s_run[at, :] * jnp.exp2(old - new) + sum(jnp.exp2(v - new) for v in t)

    def handle(entry):
        whose, da, db = entry
        if whose == "theirs":
            k = theirs(da, db)
            wait_shard(k)
            return k
        k = mine(da, db)
        if da == 0 and db == 0:
            return k
        wait_shard(k)
        if db == 0:
            for step in (1, 3, 2):
                send_shard(k, mine(0, step))
        send_shard(k, partner)
        return k

    near = [(1, 0), (3, 0), (0, 1), (0, 3), (2, 0), (0, 2)]
    later = [(a, b) for b in (1, 3, 2) for a in (1, 3, 2)]
    later.sort(key=lambda ab: (ab[0] == 2) + (ab[1] == 2))
    order = [("mine", 0, 0), ("theirs", 0, 0)]
    order += [("mine",) + ab for ab in near] + [("theirs",) + ab for ab in near]
    for i in range(0, len(later), 3):
        order += [("mine",) + ab for ab in later[i : i + 3]]
        order += [("theirs",) + ab for ab in later[i : i + 3]]

    stages = (stage_a, stage_b)
    before = None
    for n in range(0, TILES, 2):
        pair = [handle(order[n]), handle(order[n + 1])]
        products(pair, stages[(n // 2) % 2])
        if n == 0:
            wait_potential(0)
        else:
            update(before, stages[(n // 2 + 1) % 2])
        before = pair
    update(before, stages[(TILES // 2 + 1) % 2])

    def exchange_rows(iteration):
        for step in range(1, REPS):
            to = (rep + step) % REPS
            pltpu.make_async_remote_copy(
                src_ref=row_part.at[iteration, rep],
                dst_ref=row_part.at[iteration, rep],
                send_sem=row_send.at[iteration],
                recv_sem=row_recv.at[iteration],
                device_id={"rep": to},
                device_id_type=MESH,
            ).start()
        view = row_part.at[iteration, pl.ds(0, REPS - 1)]
        pltpu.make_async_copy(view, view, row_recv.at[iteration]).wait()
        return [row_part[iteration, i] for i in range(REPS)]

    def spread_rows(values):
        for q in range(chunks):
            b_col[q * LANES : (q + 1) * LANES, :] = jnp.broadcast_to(
                values[q : q + 1, :], (LANES, LANES)
            ).T

    for q in range(chunks):
        at = slice(q * LANES, (q + 1) * LANES)
        m = m_run[at, :].T
        s = s_run[at, :].T
        peak = jnp.max(m, axis=0, keepdims=True)
        total = jnp.sum(s * jnp.exp2(m - peak), axis=0, keepdims=True)
        row_part[0, rep, q : q + 1, :] = peak + jnp.log2(total)
    parts = exchange_rows(0)
    peak = functools.reduce(jnp.maximum, parts)
    total = sum(jnp.exp2(v - peak) for v in parts)
    b = LOG2E * row_logw[...] - (peak + jnp.log2(total))
    spread_rows(b)

    groups = LANES // 8

    def log_columns(k):
        bias = bias_of(k)
        for i in range(halves):
            lanes = slice(i * LANES, (i + 1) * LANES)
            peak = jnp.full((8, LANES), NEG, jnp.float32)
            total = jnp.zeros((8, LANES), jnp.float32)
            for q in range(chunks):
                at = slice(q * LANES, (q + 1) * LANES)
                t = prod[k, at, lanes] + b_col[at, :]
                prod[k, at, lanes] = t
                t = t.reshape(groups, 8, LANES)
                new = jnp.maximum(peak, jnp.max(t, axis=0))
                total = total * jnp.exp2(peak - new) + jnp.sum(jnp.exp2(t - new[None]), axis=0)
                peak = new
            top = jnp.max(peak, axis=0, keepdims=True)
            total = jnp.sum(total * jnp.exp2(peak - top), axis=0, keepdims=True)
            col_part[0, k, :, lanes] = top + jnp.log2(total) + bias

    def sum_columns(k):
        for i in range(halves):
            lanes = slice(i * LANES, (i + 1) * LANES)
            total = jnp.zeros((8, LANES), jnp.float32)
            for q in range(chunks):
                at = slice(q * LANES, (q + 1) * LANES)
                t = prod[k, at, lanes] * b_col[at, :]
                total = total + jnp.sum(t.reshape(groups, 8, LANES), axis=0)
            col_part[1, k, :, lanes] = jnp.sum(total, axis=0, keepdims=True)

    def column_pass(iteration, visit):
        def one(step, carry):
            k = peer(step)
            visit(k)
            pltpu.make_async_remote_copy(
                src_ref=col_part.at[iteration, k],
                dst_ref=col_in.at[iteration, step],
                send_sem=col_send.at[iteration],
                recv_sem=col_recv.at[iteration],
                device_id={"tile": k},
                device_id_type=MESH,
            ).start()
            return carry

        lax.fori_loop(0, TILES - 1, one, 0)
        visit(me)
        col_in[iteration, TILES - 1] = col_part[iteration, me]
        view = col_in.at[iteration, pl.ds(0, TILES - 1)]
        pltpu.make_async_copy(view, view, col_recv.at[iteration]).wait()
        return col_in[iteration]

    parts = column_pass(0, log_columns)
    peak = jnp.max(parts, axis=0)
    total = jnp.sum(jnp.exp2(parts - peak[None]), axis=0)
    a = LOG2E * col_logw[...] - (peak + jnp.log2(total))
    a_all[1, me] = a
    send_potential(1)
    wait_potential(1)

    def spread(k, carry):
        a_wide[k] = jnp.broadcast_to(a_all[1, k] + bias_of(k), (8, shard))
        return carry

    lax.fori_loop(0, TILES, spread, 0)
    step_rows = 16

    def plan_rows(step, carry):
        at = pl.ds(pl.multiple_of(step * step_rows, step_rows), step_rows)
        total = jnp.zeros((step_rows // 8, 8, LANES), jnp.float32)
        for k in range(TILES):
            t = jnp.exp2(prod[k, at, :].reshape(step_rows // 8, 8, shard) + a_wide[k][None])
            prod[k, at, :] = t.reshape(step_rows, shard)
            total = total + sum(t[:, :, i * LANES : (i + 1) * LANES] for i in range(halves))
        s_run[at, :] = total.reshape(step_rows, LANES)
        return carry

    lax.fori_loop(0, rows // step_rows, plan_rows, 0)
    for q in range(chunks):
        at = slice(q * LANES, (q + 1) * LANES)
        row_part[1, rep, q : q + 1, :] = jnp.sum(s_run[at, :].T, axis=0, keepdims=True)
    total = sum(exchange_rows(1))
    scale = jnp.exp2(LOG2E * row_logw[...]) / total
    spread_rows(scale)
    b = b + LOG2E * row_logw[...] - jnp.log2(total)

    total = jnp.sum(column_pass(1, sum_columns), axis=0)
    a = a + LOG2E * col_logw[...] - jnp.log2(total)

    row_out[...] = row_sq[...] / depth + dual_scale * b
    col_out[...] = own_sq / depth + dual_scale * a

    view = tgt.at[pl.ds(0, TILES - 1)]
    pltpu.make_async_copy(view, view, gather_send.at[0]).wait()
    for iteration in range(2):
        view = a_all.at[iteration, pl.ds(0, TILES - 1)]
        pltpu.make_async_copy(view, view, a_send.at[iteration]).wait()
        view = row_part.at[iteration, pl.ds(0, REPS - 1)]
        pltpu.make_async_copy(view, view, row_send.at[iteration]).wait()
        view = col_part.at[iteration, pl.ds(0, TILES - 1)]
        pltpu.make_async_copy(view, view, col_send.at[iteration]).wait()


def per_device(source, target, row_logw, col_logw, support):
    rows, depth = source.shape
    shard = target.shape[0]
    vmem = pl.BlockSpec(memory_space=pltpu.VMEM)
    f32 = jnp.float32
    row_dual, col_dual = pl.pallas_call(
        kernel,
        out_shape=(
            jax.ShapeDtypeStruct((rows // LANES, LANES), f32),
            jax.ShapeDtypeStruct((1, shard), f32),
        ),
        in_specs=[pl.BlockSpec(memory_space=pl.ANY)] * 5,
        out_specs=(vmem, vmem),
        scratch_shapes=[
            pltpu.VMEM((rows, depth), source.dtype),
            pltpu.VMEM((TILES, shard, depth), target.dtype),
            pltpu.VMEM((rows // LANES, LANES), f32),
            pltpu.VMEM((1, shard), f32),
            pltpu.SMEM(support.shape, support.dtype),
            pltpu.VMEM((TILES, rows, shard), f32),
            pltpu.VMEM((2, rows, shard), f32),
            pltpu.VMEM((2, rows, shard), f32),
            pltpu.VMEM((rows, LANES), f32),
            pltpu.VMEM((rows, LANES), f32),
            pltpu.VMEM((rows, LANES), f32),
            pltpu.VMEM((2, TILES, 1, shard), f32),
            pltpu.VMEM((TILES, 8, shard), f32),
            pltpu.VMEM((rows // LANES, LANES), f32),
            pltpu.VMEM((2, REPS, rows // LANES, LANES), f32),
            pltpu.VMEM((2, TILES, 1, shard), f32),
            pltpu.VMEM((2, TILES, 1, shard), f32),
            pltpu.SemaphoreType.DMA((5,)),
            pltpu.SemaphoreType.DMA((1,)),
            pltpu.SemaphoreType.DMA((TILES,)),
            pltpu.SemaphoreType.DMA((2,)),
            pltpu.SemaphoreType.DMA((2,)),
            pltpu.SemaphoreType.DMA((2,)),
            pltpu.SemaphoreType.DMA((2,)),
            pltpu.SemaphoreType.DMA((2,)),
            pltpu.SemaphoreType.DMA((2,)),
        ],
        compiler_params=pltpu.CompilerParams(
            collective_id=0, has_side_effects=True, vmem_limit_bytes=63 * 1024 * 1024
        ),
        name="sinkhorn",
    )(
        source,
        target,
        row_logw.reshape(rows // LANES, LANES),
        col_logw.reshape(1, shard),
        support,
    )
    return row_dual.reshape(rows), col_dual.reshape(shard)


def solution(mesh):
    placed = (P("tile", None), P(("rep", "tile"), None), P("tile"), P(("rep", "tile")), P())
    return jax.shard_map(
        per_device,
        mesh=mesh,
        in_specs=placed,
        out_specs=(P("tile"), P(("rep", "tile"))),
        check_vma=False,
    )
```

```python
import functools
import math

import jax
import jax.numpy as jnp
from jax import lax
from jax.experimental import pallas as pl
from jax.experimental.pallas import tpu as pltpu
from jax.sharding import PartitionSpec as P

MESH = pl.DeviceIdType.MESH
EPS = 0.1
NEG = -1e30
LOG2E = 1.0 / math.log(2.0)
LN2 = math.log(2.0)
NX = 4
TILES = 2 * NX * NX
GROUP = TILES // 2
REPS = 4
LANES = 128


def kernel(
    source_hbm,
    target_hbm,
    row_logw_hbm,
    col_logw_hbm,
    support_hbm,
    row_out,
    col_out,
    src,
    tgt,
    row_logw,
    col_logw,
    support,
    prod,
    stage_a,
    stage_b,
    m_run,
    s_run,
    b_col,
    b_keep,
    a_all,
    a_wide,
    row_sq,
    row_part,
    col_part,
    col_in,
    local_sem,
    logw_sem,
    src_send,
    src_recv,
    gather_send,
    gather_recv,
    a_send,
    a_recv,
    row_send,
    row_recv,
    col_send,
    col_recv,
):
    rows = src.shape[1]
    shard = col_logw.shape[1]
    depth = src.shape[2]
    blocks = TILES * shard // rows
    per_block = TILES // blocks
    chunks = rows // LANES
    halves = shard // LANES
    me = lax.axis_index("tile")
    rep = lax.axis_index("rep")
    core = me % 2
    x = me // (2 * NX)
    z = (me // 2) % NX
    half = x // 2
    xl = x % 2
    base = half * GROUP
    slot = me - base
    partner = me + 1 - 2 * core
    across = ((NX - 1 - x) * NX + z) * 2 + core
    row_tiles = [me * (1 - half) + across * half, across * (1 - half) + me * half]
    score_scale = 2.0 * LOG2E / (depth * EPS)
    square_scale = LOG2E / (depth * EPS)
    dual_scale = EPS * LN2

    zs = [(z + i) % NX for i in range(NX)]
    xls = [xl, 1 - xl]

    def place(dx, dz, of):
        return (xls[dx] * NX + zs[dz]) * 2 + of

    def mine(dx, dz):
        return place(dx, dz, core)

    def theirs(dx, dz):
        return place(dx, dz, 1 - core)

    def chip(step):
        m = NX - 1 - step % NX
        dz = m + m // 2 - 2 * (m // 3)
        return (((xl + 1 - step // NX) % 2) * NX + (z + dz) % NX) * 2

    def each_chip(visit):
        def one(step, at):
            visit(step, at)
            return chip(step + 1)

        lax.fori_loop(0, GROUP // 2 - 1, one, chip(0))

    def to_others(start):
        def both(step, at):
            start(2 * step, at + core)
            start(2 * step + 1, at + 1 - core)

        each_chip(both)
        start(GROUP - 2, slot + 1 - 2 * core)

    row_peers = [{"tile": me, "rep": (rep + i) % REPS} for i in range(1, REPS)]
    row_peers += [{"tile": across, "rep": (rep + i) % REPS} for i in range(REPS)]

    loads = [
        pltpu.make_async_copy(target_hbm, tgt.at[slot, pl.ds(0, shard)], local_sem.at[0]),
        pltpu.make_async_copy(source_hbm, src.at[half], local_sem.at[1]),
        pltpu.make_async_copy(support_hbm, support, local_sem.at[2]),
        pltpu.make_async_copy(row_logw_hbm, row_logw.at[half], local_sem.at[3]),
        pltpu.make_async_copy(col_logw_hbm, col_logw, local_sem.at[4]),
    ]
    for load in loads:
        load.start()

    barrier = pltpu.get_barrier_semaphore()

    def greet(message, at):
        pl.semaphore_signal(
            barrier, inc=1, device_id={"tile": base + at}, device_id_type=MESH
        )

    to_others(greet)
    for peer in row_peers:
        pl.semaphore_signal(barrier, inc=1, device_id=peer, device_id_type=MESH)

    loads[0].wait()
    own = tgt[slot, :shard].astype(jnp.float32)
    own_sq = jnp.sum((own * own).T, axis=0, keepdims=True)
    rest = -square_scale * own_sq
    parts = []
    for _ in range(3):
        parts.append(rest.astype(jnp.bfloat16))
        rest = rest - parts[-1].astype(jnp.float32)
    extra = tgt.shape[1] - shard
    tgt[slot, shard:] = jnp.concatenate(
        parts + [jnp.zeros((extra - 3, depth), jnp.bfloat16)], axis=0
    )

    pl.semaphore_wait(barrier, GROUP - 1 + len(row_peers))

    quarter = rows // REPS

    def rows_at(i):
        return pl.ds(pl.multiple_of((rep + i) % REPS * quarter, quarter), quarter)

    def send_rows(i, sem):
        pltpu.make_async_remote_copy(
            src_ref=source_hbm.at[rows_at(i)],
            dst_ref=src.at[half, rows_at(i)],
            send_sem=src_send.at[sem],
            recv_sem=src_recv.at[(rep + i) % REPS],
            device_id={"tile": across},
            device_id_type=MESH,
        ).start()

    def wait_rows(i):
        view = src.at[1 - half, rows_at(i)]
        pltpu.make_async_copy(view, view, src_recv.at[(rep + i) % REPS]).wait()

    def pass_rows(to):
        view = src.at[1 - half, rows_at(0)]
        pltpu.make_async_remote_copy(
            src_ref=view,
            dst_ref=view,
            send_sem=src_send.at[1],
            recv_sem=src_recv.at[rep],
            device_id={"rep": (rep + to) % REPS},
            device_id_type=MESH,
        ).start()

    def send_shard(k, to):
        pltpu.make_async_remote_copy(
            src_ref=tgt.at[k],
            dst_ref=tgt.at[k],
            send_sem=gather_send.at[0],
            recv_sem=gather_recv.at[k],
            device_id={"tile": base + to},
            device_id_type=MESH,
        ).start()

    def wait_shard(k):
        pltpu.make_async_copy(tgt.at[k], tgt.at[k], gather_recv.at[k]).wait()

    partner_slot = slot + 1 - 2 * core
    send_rows(0, 0)
    send_shard(slot, mine(1, 0))
    for dz in (1, 3, 2):
        send_shard(slot, mine(0, dz))
    send_shard(slot, partner_slot)
    logw_copy = pltpu.make_async_remote_copy(
        src_ref=row_logw_hbm,
        dst_ref=row_logw.at[half],
        send_sem=logw_sem.at[0],
        recv_sem=logw_sem.at[1],
        device_id={"tile": across},
        device_id_type=MESH,
    )
    logw_copy.start()

    def share_potential():
        def start(message, to):
            pltpu.make_async_remote_copy(
                src_ref=a_all.at[slot],
                dst_ref=a_all.at[slot],
                send_sem=a_send.at[0],
                recv_sem=a_recv.at[0],
                device_id={"tile": base + to},
                device_id_type=MESH,
            ).start()

        to_others(start)
        view = a_all.at[pl.ds(0, GROUP - 1)]
        pltpu.make_async_copy(view, view, a_recv.at[0]).wait()

    def bias_of(i, k):
        tile = row_tiles[0] * (1 - i) + row_tiles[1] * i
        live = support[tile, rep * blocks + (base + k) // per_block]
        return (1.0 - live.astype(jnp.float32)) * NEG

    for load in loads[1:]:
        load.wait()

    m_run[...] = jnp.full(m_run.shape, NEG, jnp.float32)
    s_run[...] = jnp.zeros(s_run.shape, jnp.float32)
    for q in range(chunks):
        cells = src[half, q * LANES : (q + 1) * LANES, :].astype(jnp.float32)
        sq = cells * cells
        sq = sum(sq[:, i * LANES : (i + 1) * LANES] for i in range(depth // LANES))
        row_sq[q : q + 1, :] = jnp.sum(sq.T, axis=0, keepdims=True)

    view = src.at[0, pl.ds(0, quarter)]
    pltpu.make_async_copy(view, view, src_send.at[0]).wait()
    send_rows(2, 1)

    def against(left, right):
        return lax.dot_general(
            left, right, (((1,), (1,)), ((), ())), preferred_element_type=jnp.float32
        )

    def products(i, pair, stage):
        for n, k in enumerate(pair):
            for r in range(0, rows, 512):
                stage[n, r : r + 512, :] = against(src[i, r : r + 512, :], tgt[k, :shard])

    def column_term(i, k):
        parts = tgt[k, shard:].astype(jnp.float32)
        return parts[0:1] + parts[1:2] + parts[2:3] + bias_of(i, k)

    def update(i, pair, stage, terms):
        step = 32
        for r in range(0, rows, step):
            at = slice(r, r + step)
            t = []
            for n, k in enumerate(pair):
                p = stage[n, at, :] * score_scale
                prod[k, i, at, :] = p
                t.extend(
                    p[:, h * LANES : (h + 1) * LANES] + terms[n][:, h * LANES : (h + 1) * LANES]
                    for h in range(halves)
                )
            old = m_run[i, at, :]
            new = functools.reduce(jnp.maximum, t, old)
            m_run[i, at, :] = new
            s_run[i, at, :] = s_run[i, at, :] * jnp.exp2(old - new) + sum(
                jnp.exp2(v - new) for v in t
            )

    def handle(entry):
        whose, dx, dz = entry
        if whose == "theirs":
            k = theirs(dx, dz)
            wait_shard(k)
            return k
        k = mine(dx, dz)
        if dx == 0 and dz == 0:
            return k
        wait_shard(k)
        if dx == 1 and dz == 0:

            @pl.when(core == 0)
            def _():
                for step in (1, 3, 2):
                    send_shard(k, mine(0, step))

        elif dx == 0:

            @pl.when(core == 1)
            def _():
                send_shard(k, mine(1, 0))

        send_shard(k, partner_slot)
        return k

    def m(dx, dz):
        return ("mine", dx, dz)

    def t(dx, dz):
        return ("theirs", dx, dz)

    pairs = [
        (m(0, 0), t(0, 0)),
        (m(1, 0), m(0, 1)),
        (m(0, 3), m(0, 2)),
        (t(1, 0), t(0, 1)),
        (t(0, 3), t(0, 2)),
        (m(1, 1), m(1, 3)),
        (t(1, 1), t(1, 3)),
        (m(1, 2), t(1, 2)),
    ]
    steps = [(0, 0), (1, 0), (2, 0), (3, 0), (4, 0), (0, 1), (1, 1), (5, 0)]
    steps += [(2, 1), (3, 1), (6, 0), (4, 1), (5, 1), (7, 0), (6, 1), (7, 1)]
    stages = (stage_a, stage_b)
    ready = {}
    before = None
    for n in range(len(steps) + 1):
        now = None
        if n < len(steps):
            which, other = steps[n]
            if which not in ready:
                ready[which] = [handle(entry) for entry in pairs[which]]
            if n == 1:
                wait_rows(0)
                pass_rows(1)
                pass_rows(3)
            if n == 5:
                for i in (2, 1, 3):
                    wait_rows(i)
            i = (1 - half) if other else half
            now = (i, ready[which])
        if before is not None:
            terms = [column_term(before[0], k) for k in before[1]]
        if now is not None:
            products(now[0], now[1], stages[n % 2])
        if before is not None:
            update(before[0], before[1], stages[(n + 1) % 2], terms)
        before = now

    row_slot = half * REPS + rep

    def exchange_rows(iteration):
        for peer in row_peers:
            pltpu.make_async_remote_copy(
                src_ref=row_part.at[iteration, row_slot],
                dst_ref=row_part.at[iteration, row_slot],
                send_sem=row_send.at[iteration],
                recv_sem=row_recv.at[iteration],
                device_id=peer,
                device_id_type=MESH,
            ).start()
        view = row_part.at[iteration, pl.ds(0, len(row_peers))]
        pltpu.make_async_copy(view, view, row_recv.at[iteration]).wait()
        return [row_part[iteration, i] for i in range(2 * REPS)]

    def spread_rows(values):
        for i in range(2):
            for q in range(chunks):
                b_col[i, q * LANES : (q + 1) * LANES, :] = jnp.broadcast_to(
                    values[i, q : q + 1, :], (LANES, LANES)
                ).T

    for i in range(2):
        for q in range(chunks):
            at = slice(q * LANES, (q + 1) * LANES)
            m = m_run[i, at, :].T
            s = s_run[i, at, :].T
            peak = jnp.max(m, axis=0, keepdims=True)
            total = jnp.sum(s * jnp.exp2(m - peak), axis=0, keepdims=True)
            row_part[0, row_slot, i, q : q + 1, :] = peak + jnp.log2(total)
    parts = exchange_rows(0)
    peak = functools.reduce(jnp.maximum, parts)
    total = sum(jnp.exp2(v - peak) for v in parts)
    logw_copy.wait()
    b = LOG2E * row_logw[...] - (peak + jnp.log2(total))
    spread_rows(b)

    groups = LANES // 8

    def tree(op, v):
        while v.shape[0] > 1:
            n = v.shape[0] // 2
            v = op(v[:n], v[n:])
        return v[0]

    def lane_tiles(v):
        return [v[..., i * LANES : (i + 1) * LANES] for i in range(halves)]

    def log_columns(pair):
        tiles = [(k, slice(i * LANES, (i + 1) * LANES)) for k in pair for i in range(halves)]
        parts = []
        for block in range(2):
            biases = [bias_of(block, k) for k in pair]
            peaks = [jnp.full((8, LANES), NEG, jnp.float32)] * len(tiles)
            totals = [jnp.zeros((8, LANES), jnp.float32)] * len(tiles)
            for q in range(chunks):
                at = slice(q * LANES, (q + 1) * LANES)
                row_term = b_col[block, at, :]
                for n, (k, lanes) in enumerate(tiles):
                    t = prod[k, block, at, lanes] + row_term
                    prod[k, block, at, lanes] = t
                    t = t.reshape(groups, 8, LANES)
                    new = jnp.maximum(peaks[n], tree(jnp.maximum, t))
                    totals[n] = totals[n] * jnp.exp2(peaks[n] - new) + tree(
                        jnp.add, jnp.exp2(t - new[None])
                    )
                    peaks[n] = new
            for n in range(len(tiles)):
                top = jnp.max(peaks[n], axis=0, keepdims=True)
                total = jnp.sum(totals[n] * jnp.exp2(peaks[n] - top), axis=0, keepdims=True)
                parts.append(top + jnp.log2(total) + biases[n // halves])
        for n, (k, lanes) in enumerate(tiles):
            one, two = parts[n], parts[n + len(tiles)]
            top = jnp.maximum(one, two)
            col_part[0, k, :, lanes] = top + jnp.log2(jnp.exp2(one - top) + jnp.exp2(two - top))

    def sum_columns(pair):
        tiles = [(k, slice(i * LANES, (i + 1) * LANES)) for k in pair for i in range(halves)]
        totals = [jnp.zeros((4, 8, LANES), jnp.float32)] * len(tiles)
        few = 64
        for block in range(2):
            for r in range(0, rows, few):
                at = slice(r, r + few)
                row_term = b_col[block, at, :]
                for n, (k, lanes) in enumerate(tiles):
                    t = (prod[k, block, at, lanes] * row_term).reshape(2, 4, 8, LANES)
                    totals[n] = totals[n] + (t[0] + t[1])
        for n, (k, lanes) in enumerate(tiles):
            col_part[1, k, :, lanes] = jnp.sum(tree(jnp.add, totals[n]), axis=0, keepdims=True)

    def column_pass(iteration, visit):
        def start(message, k):
            pltpu.make_async_remote_copy(
                src_ref=col_part.at[iteration, k],
                dst_ref=col_in.at[iteration, message],
                send_sem=col_send.at[iteration],
                recv_sem=col_recv.at[iteration],
                device_id={"tile": base + k},
                device_id_type=MESH,
            ).start()

        def both(step, at):
            visit((at, at + 1))
            start(2 * step, at + core)
            start(2 * step + 1, at + 1 - core)

        each_chip(both)
        visit((slot - core, slot - core + 1))
        start(GROUP - 2, partner_slot)
        col_in[iteration, GROUP - 1] = col_part[iteration, slot]
        view = col_in.at[iteration, pl.ds(0, GROUP - 1)]
        pltpu.make_async_copy(view, view, col_recv.at[iteration]).wait()
        return col_in[iteration]

    parts = column_pass(0, log_columns)
    peak = jnp.max(parts, axis=0)
    total = jnp.sum(jnp.exp2(parts - peak[None]), axis=0)
    a = LOG2E * col_logw[...] - (peak + jnp.log2(total))
    a_all[slot] = a
    share_potential()

    def spread(k, carry):
        for i in range(2):
            a_wide[i, k] = jnp.broadcast_to(a_all[k] + bias_of(i, k), (8, shard))
        return carry

    lax.fori_loop(0, GROUP, spread, 0)
    step_rows = 32

    def plan_rows(step, carry):
        block = step // (rows // step_rows)
        at = pl.ds(
            pl.multiple_of(step % (rows // step_rows) * step_rows, step_rows), step_rows
        )
        totals = [jnp.zeros((step_rows // 8, 8, LANES), jnp.float32)] * 2
        for k in range(GROUP):
            t = jnp.exp2(
                prod[k, block, at, :].reshape(step_rows // 8, 8, shard) + a_wide[block, k][None]
            )
            prod[k, block, at, :] = t.reshape(step_rows, shard)
            totals[k % 2] = totals[k % 2] + sum(lane_tiles(t))
        s_run[block, at, :] = sum(totals).reshape(step_rows, LANES)
        return carry

    lax.fori_loop(0, 2 * rows // step_rows, plan_rows, 0)
    for i in range(2):
        for q in range(chunks):
            at = slice(q * LANES, (q + 1) * LANES)
            row_part[1, row_slot, i, q : q + 1, :] = jnp.sum(
                s_run[i, at, :].T, axis=0, keepdims=True
            )
    total = sum(exchange_rows(1))
    scale = jnp.exp2(LOG2E * row_logw[...]) / total
    spread_rows(scale)
    b_keep[...] = b + LOG2E * row_logw[...] - jnp.log2(total)

    total = jnp.sum(column_pass(1, sum_columns), axis=0)
    a = a + LOG2E * col_logw[...] - jnp.log2(total)

    row_out[...] = row_sq[...] / depth + dual_scale * b_keep[half]
    col_out[...] = own_sq / depth + dual_scale * a

    view = tgt.at[pl.ds(0, GROUP - 1)]
    pltpu.make_async_copy(view, view, gather_send.at[0]).wait()
    view = src.at[0, pl.ds(0, 3 * quarter)]
    pltpu.make_async_copy(view, view, src_send.at[1]).wait()
    view = a_all.at[pl.ds(0, GROUP - 1)]
    pltpu.make_async_copy(view, view, a_send.at[0]).wait()
    for iteration in range(2):
        view = row_part.at[iteration, pl.ds(0, len(row_peers))]
        pltpu.make_async_copy(view, view, row_send.at[iteration]).wait()
        view = col_part.at[iteration, pl.ds(0, GROUP - 1)]
        pltpu.make_async_copy(view, view, col_send.at[iteration]).wait()


def per_device(source, target, row_logw, col_logw, support):
    rows, depth = source.shape
    shard = target.shape[0]
    vmem = pl.BlockSpec(memory_space=pltpu.VMEM)
    f32 = jnp.float32
    row_dual, col_dual = pl.pallas_call(
        kernel,
        out_shape=(
            jax.ShapeDtypeStruct((rows // LANES, LANES), f32),
            jax.ShapeDtypeStruct((1, shard), f32),
        ),
        in_specs=[pl.BlockSpec(memory_space=pl.ANY)] * 5,
        out_specs=(vmem, vmem),
        scratch_shapes=[
            pltpu.VMEM((2, rows, depth), source.dtype),
            pltpu.VMEM((GROUP, shard + 16, depth), target.dtype),
            pltpu.VMEM((2, rows // LANES, LANES), f32),
            pltpu.VMEM((1, shard), f32),
            pltpu.SMEM(support.shape, support.dtype),
            pltpu.VMEM((GROUP, 2, rows, shard), f32),
            pltpu.VMEM((2, rows, shard), f32),
            pltpu.VMEM((2, rows, shard), f32),
            pltpu.VMEM((2, rows, LANES), f32),
            pltpu.VMEM((2, rows, LANES), f32),
            pltpu.VMEM((2, rows, LANES), f32),
            pltpu.VMEM((2, rows // LANES, LANES), f32),
            pltpu.VMEM((GROUP, 1, shard), f32),
            pltpu.VMEM((2, GROUP, 8, shard), f32),
            pltpu.VMEM((rows // LANES, LANES), f32),
            pltpu.VMEM((2, 2 * REPS, 2, rows // LANES, LANES), f32),
            pltpu.VMEM((2, GROUP, 1, shard), f32),
            pltpu.VMEM((2, GROUP, 1, shard), f32),
            pltpu.SemaphoreType.DMA((5,)),
            pltpu.SemaphoreType.DMA((2,)),
            pltpu.SemaphoreType.DMA((2,)),
            pltpu.SemaphoreType.DMA((REPS,)),
            pltpu.SemaphoreType.DMA((1,)),
            pltpu.SemaphoreType.DMA((GROUP,)),
            pltpu.SemaphoreType.DMA((1,)),
            pltpu.SemaphoreType.DMA((1,)),
            pltpu.SemaphoreType.DMA((2,)),
            pltpu.SemaphoreType.DMA((2,)),
            pltpu.SemaphoreType.DMA((2,)),
            pltpu.SemaphoreType.DMA((2,)),
        ],
        compiler_params=pltpu.CompilerParams(
            collective_id=0, has_side_effects=True, vmem_limit_bytes=63 * 1024 * 1024
        ),
        name="sinkhorn",
    )(
        source,
        target,
        row_logw.reshape(rows // LANES, LANES),
        col_logw.reshape(1, shard),
        support,
    )
    return row_dual.reshape(rows), col_dual.reshape(shard)


def solution(mesh):
    placed = (P("tile", None), P(("rep", "tile"), None), P("tile"), P(("rep", "tile")), P())
    return jax.shard_map(
        per_device,
        mesh=mesh,
        in_specs=placed,
        out_specs=(P("tile"), P(("rep", "tile"))),
        check_vma=False,
    )
```

```python
import functools
import math

import jax
import jax.numpy as jnp
from jax import lax
from jax.experimental import pallas as pl
from jax.experimental.pallas import tpu as pltpu
from jax.sharding import PartitionSpec as P

MESH = pl.DeviceIdType.MESH
EPS = 0.1
NEG = -1e30
LOG2E = 1.0 / math.log(2.0)
LN2 = math.log(2.0)
NX = 4
TILES = 2 * NX * NX
GROUP = TILES // 2
REPS = 4
LANES = 128


def kernel(
    source_hbm,
    target_hbm,
    row_logw_hbm,
    col_logw_hbm,
    support_hbm,
    row_out,
    col_out,
    src,
    tgt,
    row_logw,
    col_logw,
    support,
    prod,
    stage_a,
    stage_b,
    m_run,
    s_run,
    b_col,
    b_keep,
    a_all,
    a_wide,
    row_sq,
    row_part,
    col_part,
    col_in,
    local_sem,
    logw_sem,
    src_send,
    src_recv,
    gather_send,
    gather_recv,
    a_send,
    a_recv,
    row_send,
    row_recv,
    col_send,
    col_recv,
):
    rows = src.shape[1]
    shard = col_logw.shape[1]
    depth = src.shape[2]
    blocks = TILES * shard // rows
    per_block = TILES // blocks
    chunks = rows // LANES
    halves = shard // LANES
    me = lax.axis_index("tile")
    rep = lax.axis_index("rep")
    core = me % 2
    x = me // (2 * NX)
    z = (me // 2) % NX
    half = x // 2
    xl = x % 2
    base = half * GROUP
    slot = me - base
    partner = me + 1 - 2 * core
    across = ((NX - 1 - x) * NX + z) * 2 + core
    row_tiles = [me * (1 - half) + across * half, across * (1 - half) + me * half]
    score_scale = 2.0 * LOG2E / (depth * EPS)
    square_scale = LOG2E / (depth * EPS)
    dual_scale = EPS * LN2

    zs = [(z + i) % NX for i in range(NX)]
    xls = [xl, 1 - xl]

    def place(dx, dz, of):
        return (xls[dx] * NX + zs[dz]) * 2 + of

    def mine(dx, dz):
        return place(dx, dz, core)

    def theirs(dx, dz):
        return place(dx, dz, 1 - core)

    def chip(step):
        m = NX - 1 - step % NX
        dz = m + m // 2 - 2 * (m // 3)
        return (((xl + 1 - step // NX) % 2) * NX + (z + dz) % NX) * 2

    def each_chip(visit):
        def one(step, at):
            visit(step, at)
            return chip(step + 1)

        lax.fori_loop(0, GROUP // 2 - 1, one, chip(0))

    def to_others(start):
        def both(step, at):
            start(2 * step, at + core)
            start(2 * step + 1, at + 1 - core)

        each_chip(both)
        start(GROUP - 2, slot + 1 - 2 * core)

    def reached(j, c):
        return (j + 16 - c) // 16

    def pair_at(p):
        turn = (p + 1) % 3
        dz = (1 + 2 * turn - 3 * (turn // 2)) * reached(p, 2)
        dx = reached(p, 1) - reached(p, 2) + reached(p, 5)
        return (((xl + dx) % 2) * NX + (z + dz) % NX) * 2

    row_peers = [{"tile": me, "rep": (rep + i) % REPS} for i in range(1, REPS)]
    row_peers += [{"tile": across, "rep": (rep + i) % REPS} for i in range(REPS)]

    loads = [
        pltpu.make_async_copy(target_hbm, tgt.at[slot, pl.ds(0, shard)], local_sem.at[0]),
        pltpu.make_async_copy(source_hbm, src.at[half], local_sem.at[1]),
        pltpu.make_async_copy(support_hbm, support, local_sem.at[2]),
        pltpu.make_async_copy(row_logw_hbm, row_logw.at[half], local_sem.at[3]),
        pltpu.make_async_copy(col_logw_hbm, col_logw, local_sem.at[4]),
    ]
    for load in loads:
        load.start()

    barrier = pltpu.get_barrier_semaphore()

    def greet(message, at):
        pl.semaphore_signal(
            barrier, inc=1, device_id={"tile": base + at}, device_id_type=MESH
        )

    to_others(greet)
    for peer in row_peers:
        pl.semaphore_signal(barrier, inc=1, device_id=peer, device_id_type=MESH)

    loads[0].wait()
    own = tgt[slot, :shard].astype(jnp.float32)
    own_sq = jnp.sum((own * own).T, axis=0, keepdims=True)
    rest = -square_scale * own_sq
    parts = []
    for _ in range(3):
        parts.append(rest.astype(jnp.bfloat16))
        rest = rest - parts[-1].astype(jnp.float32)
    extra = tgt.shape[1] - shard
    tgt[slot, shard:] = jnp.concatenate(
        parts + [jnp.zeros((extra - 3, depth), jnp.bfloat16)], axis=0
    )

    pl.semaphore_wait(barrier, GROUP - 1 + len(row_peers))

    quarter = rows // REPS

    def rows_at(i):
        return pl.ds(pl.multiple_of((rep + i) % REPS * quarter, quarter), quarter)

    def send_rows(i, sem):
        pltpu.make_async_remote_copy(
            src_ref=source_hbm.at[rows_at(i)],
            dst_ref=src.at[half, rows_at(i)],
            send_sem=src_send.at[sem],
            recv_sem=src_recv.at[(rep + i) % REPS],
            device_id={"tile": across},
            device_id_type=MESH,
        ).start()

    def wait_rows(i):
        view = src.at[1 - half, rows_at(i)]
        pltpu.make_async_copy(view, view, src_recv.at[(rep + i) % REPS]).wait()

    def pass_rows(to):
        view = src.at[1 - half, rows_at(0)]
        pltpu.make_async_remote_copy(
            src_ref=view,
            dst_ref=view,
            send_sem=src_send.at[1],
            recv_sem=src_recv.at[rep],
            device_id={"rep": (rep + to) % REPS},
            device_id_type=MESH,
        ).start()

    def send_shard(k, to):
        pltpu.make_async_remote_copy(
            src_ref=tgt.at[k],
            dst_ref=tgt.at[k],
            send_sem=gather_send.at[0],
            recv_sem=gather_recv.at[k],
            device_id={"tile": base + to},
            device_id_type=MESH,
        ).start()

    def wait_shard(k):
        pltpu.make_async_copy(tgt.at[k], tgt.at[k], gather_recv.at[k]).wait()

    partner_slot = slot + 1 - 2 * core
    send_rows(0, 0)
    send_shard(slot, mine(1, 0))
    for dz in (1, 3, 2):
        send_shard(slot, mine(0, dz))
    send_shard(slot, partner_slot)
    logw_copy = pltpu.make_async_remote_copy(
        src_ref=row_logw_hbm,
        dst_ref=row_logw.at[half],
        send_sem=logw_sem.at[0],
        recv_sem=logw_sem.at[1],
        device_id={"tile": across},
        device_id_type=MESH,
    )
    logw_copy.start()

    def share_potential():
        def start(message, to):
            step = message // 2
            near = reached(step, 3) - reached(step, 4) + reached(step, 5)
            pltpu.make_async_remote_copy(
                src_ref=a_all.at[slot],
                dst_ref=a_all.at[slot],
                send_sem=a_send.at[0],
                recv_sem=a_recv.at[1 - near],
                device_id={"tile": base + to},
                device_id_type=MESH,
            ).start()

        to_others(start)

    near_messages = 7

    def wait_potential(far):
        view = a_all.at[pl.ds(0, GROUP - 1 - near_messages if far else near_messages)]
        pltpu.make_async_copy(view, view, a_recv.at[far]).wait()

    def bias_of(i, k):
        tile = row_tiles[0] * (1 - i) + row_tiles[1] * i
        live = support[tile, rep * blocks + (base + k) // per_block]
        return (1.0 - live.astype(jnp.float32)) * NEG

    for load in loads[1:]:
        load.wait()

    m_run[...] = jnp.full(m_run.shape, NEG, jnp.float32)
    s_run[...] = jnp.zeros(s_run.shape, jnp.float32)
    for q in range(chunks):
        cells = src[half, q * LANES : (q + 1) * LANES, :].astype(jnp.float32)
        sq = cells * cells
        sq = sum(sq[:, i * LANES : (i + 1) * LANES] for i in range(depth // LANES))
        row_sq[q : q + 1, :] = jnp.sum(sq.T, axis=0, keepdims=True)

    view = src.at[0, pl.ds(0, quarter)]
    pltpu.make_async_copy(view, view, src_send.at[0]).wait()
    send_rows(2, 1)

    def against(left, right):
        return lax.dot_general(
            left, right, (((1,), (1,)), ((), ())), preferred_element_type=jnp.float32
        )

    def products(i, pair, stage):
        for n, k in enumerate(pair):
            for r in range(0, rows, 512):
                stage[n, r : r + 512, :] = against(src[i, r : r + 512, :], tgt[k, :shard])

    def column_term(i, k):
        parts = tgt[k, shard:].astype(jnp.float32)
        return parts[0:1] + parts[1:2] + parts[2:3] + bias_of(i, k)

    def update(i, pair, stage, terms):
        step = 32
        for r in range(0, rows, step):
            at = slice(r, r + step)
            t = []
            for n, k in enumerate(pair):
                p = stage[n, at, :] * score_scale
                prod[k, i, at, :] = p
                t.extend(
                    p[:, h * LANES : (h + 1) * LANES] + terms[n][:, h * LANES : (h + 1) * LANES]
                    for h in range(halves)
                )
            old = m_run[i, at, :]
            new = functools.reduce(jnp.maximum, t, old)
            m_run[i, at, :] = new
            s_run[i, at, :] = s_run[i, at, :] * jnp.exp2(old - new) + sum(
                jnp.exp2(v - new) for v in t
            )

    def receive(p):
        k = pair_at(p) + core
        wait_shard(k)

        @pl.when(core * 8 + p == 1)
        def _():
            for dz in (1, 3, 2):
                send_shard(k, mine(0, dz))

        @pl.when(core * reached(p, 2) * (1 - reached(p, 5)) == 1)
        def _():
            send_shard(k, mine(1, 0))

        send_shard(k, partner_slot)

    def receive_theirs(p):
        wait_shard(pair_at(p) + 1 - core)

    def rows_of(other):
        return half + other * (1 - 2 * half)

    def step_at(n):
        late = reached(n, 4)
        par = reached(n, 8) * (1 - half) + (late - reached(n, 12)) * half
        p = n - 8 * reached(n, 8) * (1 - half) - 4 * (late + reached(n, 12)) * half
        at = pair_at(p - reached(n, 16))
        return half + par * (1 - 2 * half), (at, at + 1)

    row_slot = half * REPS + rep

    def send_row_sums(iteration, block):
        for peer in row_peers:
            pltpu.make_async_remote_copy(
                src_ref=row_part.at[iteration, block, row_slot],
                dst_ref=row_part.at[iteration, block, row_slot],
                send_sem=row_send.at[iteration, block],
                recv_sem=row_recv.at[iteration, block],
                device_id=peer,
                device_id_type=MESH,
            ).start()

    def take_row_sums(iteration, block):
        view = row_part.at[iteration, block, pl.ds(0, len(row_peers))]
        pltpu.make_async_copy(view, view, row_recv.at[iteration, block]).wait()
        return [row_part[iteration, block, i] for i in range(2 * REPS)]

    def spread_rows(block, values):
        for q in range(chunks):
            b_col[block, q * LANES : (q + 1) * LANES, :] = jnp.broadcast_to(
                values[q : q + 1, :], (LANES, LANES)
            ).T

    def fold_log_rows(block):
        for q in range(chunks):
            at = slice(q * LANES, (q + 1) * LANES)
            m = m_run[block, at, :].T
            s = s_run[block, at, :].T
            peak = jnp.max(m, axis=0, keepdims=True)
            total = jnp.sum(s * jnp.exp2(m - peak), axis=0, keepdims=True)
            row_part[0, block, row_slot, q : q + 1, :] = peak + jnp.log2(total)
        send_row_sums(0, block)

    turns = 8
    receive_theirs(0)
    products(*step_at(0), stage_a)

    def turn(j, carry):
        @pl.when(j == 6)
        def _():
            fold_log_rows(0)

        now = step_at(2 * j)

        @pl.when(j == 0)
        def _():
            receive(1)
            wait_rows(0)
            pass_rows(1)
            pass_rows(3)
            receive(2)
            receive_theirs(1)

        @pl.when(reached(j, 1) * (1 - reached(j, 4)) == 1)
        def _():
            @pl.when(j < 3)
            def _():
                receive(2 * j + 2)

            receive_theirs(2 * j + 1)

        later = step_at(2 * j + 1)
        terms = [column_term(now[0], k) for k in now[1]]
        products(*later, stage_b)
        update(*now, stage_a, terms)

        now = later

        @pl.when(j < 3)
        def _():
            receive(2 * j + 3)
            receive_theirs(2 * j + 2)

        @pl.when(j == 3 - 2 * half)
        def _():
            for i in (2, 1, 3):
                wait_rows(i)

        later = step_at(2 * j + 2)
        terms = [column_term(now[0], k) for k in now[1]]
        products(*later, stage_a)
        update(*now, stage_b, terms)
        return carry

    lax.fori_loop(0, turns, turn, 0)
    fold_log_rows(1)
    logw_copy.wait()

    def finish_log_rows(block):
        parts = take_row_sums(0, block)
        peak = functools.reduce(jnp.maximum, parts)
        total = sum(jnp.exp2(v - peak) for v in parts)
        b = LOG2E * row_logw[block] - (peak + jnp.log2(total))
        b_keep[block] = b
        spread_rows(block, b)

    groups = LANES // 8

    def tree(op, v):
        while v.shape[0] > 1:
            n = v.shape[0] // 2
            v = op(v[:n], v[n:])
        return v[0]

    def lane_tiles(v):
        return [v[..., i * LANES : (i + 1) * LANES] for i in range(halves)]

    def tiles_of(pair):
        return [(k, slice(i * LANES, (i + 1) * LANES)) for k in pair for i in range(halves)]

    def log_columns(pair, block):
        tiles = tiles_of(pair)
        biases = [bias_of(block, k) for k in pair]
        peaks = [jnp.full((8, LANES), NEG, jnp.float32)] * len(tiles)
        totals = [jnp.zeros((8, LANES), jnp.float32)] * len(tiles)
        for q in range(chunks):
            at = slice(q * LANES, (q + 1) * LANES)
            row_term = b_col[block, at, :]
            for n, (k, lanes) in enumerate(tiles):
                t = prod[k, block, at, lanes] + row_term
                prod[k, block, at, lanes] = t
                t = t.reshape(groups, 8, LANES)
                new = jnp.maximum(peaks[n], tree(jnp.maximum, t))
                totals[n] = totals[n] * jnp.exp2(peaks[n] - new) + tree(
                    jnp.add, jnp.exp2(t - new[None])
                )
                peaks[n] = new
        parts = []
        for n in range(len(tiles)):
            top = jnp.max(peaks[n], axis=0, keepdims=True)
            total = jnp.sum(totals[n] * jnp.exp2(peaks[n] - top), axis=0, keepdims=True)
            parts.append(top + jnp.log2(total) + biases[n // halves])
        return parts

    def log_first(pair):
        for (k, lanes), part in zip(tiles_of(pair), log_columns(pair, 0)):
            col_part[0, k, :, lanes] = part

    def log_second(pair):
        for (k, lanes), two in zip(tiles_of(pair), log_columns(pair, 1)):
            one = col_part[0, k, :, lanes]
            top = jnp.maximum(one, two)
            col_part[0, k, :, lanes] = top + jnp.log2(jnp.exp2(one - top) + jnp.exp2(two - top))

    def sum_columns(pair, block):
        tiles = tiles_of(pair)

        def some(q, carry):
            at = pl.ds(pl.multiple_of(q * LANES, LANES), LANES)
            row_term = b_col[block, at, :]
            out = []
            for (k, lanes), total in zip(tiles, carry):
                t = (prod[k, block, at, lanes] * row_term).reshape(4, 4, 8, LANES)
                out.append(total + ((t[0] + t[1]) + (t[2] + t[3])))
            return tuple(out)

        start = (jnp.zeros((4, 8, LANES), jnp.float32),) * len(tiles)
        totals = lax.fori_loop(0, chunks, some, start, unroll=2)
        return [jnp.sum(tree(jnp.add, total), axis=0, keepdims=True) for total in totals]

    def sum_first(pair):
        for (k, lanes), part in zip(tiles_of(pair), sum_columns(pair, 0)):
            col_part[1, k, :, lanes] = part

    def sum_second(pair):
        for (k, lanes), part in zip(tiles_of(pair), sum_columns(pair, 1)):
            col_part[1, k, :, lanes] = col_part[1, k, :, lanes] + part

    def all_chips(visit):
        def one(n, carry):
            visit((2 * n, 2 * n + 1))
            return carry

        lax.fori_loop(0, GROUP // 2, one, 0)

    def column_pass(iteration, visit):
        def start(message, k):
            pltpu.make_async_remote_copy(
                src_ref=col_part.at[iteration, k],
                dst_ref=col_in.at[iteration, message],
                send_sem=col_send.at[iteration],
                recv_sem=col_recv.at[iteration],
                device_id={"tile": base + k},
                device_id_type=MESH,
            ).start()

        def both(step, at):
            visit((at, at + 1))
            start(2 * step, at + core)
            start(2 * step + 1, at + 1 - core)

        each_chip(both)
        visit((slot - core, slot - core + 1))
        start(GROUP - 2, partner_slot)
        col_in[iteration, GROUP - 1] = col_part[iteration, slot]
        view = col_in.at[iteration, pl.ds(0, GROUP - 1)]
        pltpu.make_async_copy(view, view, col_recv.at[iteration]).wait()
        return col_in[iteration]

    finish_log_rows(0)
    all_chips(log_first)
    finish_log_rows(1)
    parts = column_pass(0, log_second)
    peak = jnp.max(parts, axis=0)
    total = jnp.sum(jnp.exp2(parts - peak[None]), axis=0)
    a = LOG2E * col_logw[...] - (peak + jnp.log2(total))
    a_all[slot] = a
    share_potential()

    def spread_potential(pairs):
        for p in pairs:
            at = pair_at(p)
            for k in (at, at + 1):
                for i in range(2):
                    a_wide[i, k] = jnp.broadcast_to(a_all[k] + bias_of(i, k), (8, shard))

    step_rows = 128

    def plan_rows(block, pairs, more):
        slots = [pair_at(p) + c for p in pairs for c in range(2)]

        def some(step, carry):
            at = pl.ds(pl.multiple_of(step * step_rows, step_rows), step_rows)
            totals = [jnp.zeros((step_rows // 8, 8, LANES), jnp.float32)] * 2
            if more:
                totals[0] = s_run[block, at, :].reshape(step_rows // 8, 8, LANES)
            for n, k in enumerate(slots):
                t = jnp.exp2(
                    prod[k, block, at, :].reshape(step_rows // 8, 8, shard)
                    + a_wide[block, k][None]
                )
                prod[k, block, at, :] = t.reshape(step_rows, shard)
                totals[n % 2] = totals[n % 2] + sum(lane_tiles(t))
            s_run[block, at, :] = sum(totals).reshape(step_rows, LANES)
            return carry

        lax.fori_loop(0, rows // step_rows, some, 0)

    def fold_rows(block):
        for q in range(chunks):
            at = slice(q * LANES, (q + 1) * LANES)
            row_part[1, block, row_slot, q : q + 1, :] = jnp.sum(
                s_run[block, at, :].T, axis=0, keepdims=True
            )
        send_row_sums(1, block)

    def finish_rows(block):
        total = sum(take_row_sums(1, block))
        spread_rows(block, jnp.exp2(LOG2E * row_logw[block]) / total)
        b_keep[block] = b_keep[block] + LOG2E * row_logw[block] - jnp.log2(total)

    wait_potential(0)
    spread_potential(range(4))
    plan_rows(0, range(4), False)
    wait_potential(1)
    spread_potential(range(4, 8))
    plan_rows(0, range(4, 8), True)
    fold_rows(0)
    plan_rows(1, range(8), False)
    fold_rows(1)
    finish_rows(0)
    all_chips(sum_first)
    finish_rows(1)

    total = jnp.sum(column_pass(1, sum_second), axis=0)
    a = a + LOG2E * col_logw[...] - jnp.log2(total)

    row_out[...] = row_sq[...] / depth + dual_scale * b_keep[half]
    col_out[...] = own_sq / depth + dual_scale * a

    view = tgt.at[pl.ds(0, GROUP - 1)]
    pltpu.make_async_copy(view, view, gather_send.at[0]).wait()
    view = src.at[0, pl.ds(0, 3 * quarter)]
    pltpu.make_async_copy(view, view, src_send.at[1]).wait()
    view = a_all.at[pl.ds(0, GROUP - 1)]
    pltpu.make_async_copy(view, view, a_send.at[0]).wait()
    for iteration in range(2):
        for block in range(2):
            view = row_part.at[iteration, block, pl.ds(0, len(row_peers))]
            pltpu.make_async_copy(view, view, row_send.at[iteration, block]).wait()
        view = col_part.at[iteration, pl.ds(0, GROUP - 1)]
        pltpu.make_async_copy(view, view, col_send.at[iteration]).wait()


def per_device(source, target, row_logw, col_logw, support):
    rows, depth = source.shape
    shard = target.shape[0]
    vmem = pl.BlockSpec(memory_space=pltpu.VMEM)
    f32 = jnp.float32
    row_dual, col_dual = pl.pallas_call(
        kernel,
        out_shape=(
            jax.ShapeDtypeStruct((rows // LANES, LANES), f32),
            jax.ShapeDtypeStruct((1, shard), f32),
        ),
        in_specs=[pl.BlockSpec(memory_space=pl.ANY)] * 5,
        out_specs=(vmem, vmem),
        scratch_shapes=[
            pltpu.VMEM((2, rows, depth), source.dtype),
            pltpu.VMEM((GROUP, shard + 16, depth), target.dtype),
            pltpu.VMEM((2, rows // LANES, LANES), f32),
            pltpu.VMEM((1, shard), f32),
            pltpu.SMEM(support.shape, support.dtype),
            pltpu.VMEM((GROUP, 2, rows, shard), f32),
            pltpu.VMEM((2, rows, shard), f32),
            pltpu.VMEM((2, rows, shard), f32),
            pltpu.VMEM((2, rows, LANES), f32),
            pltpu.VMEM((2, rows, LANES), f32),
            pltpu.VMEM((2, rows, LANES), f32),
            pltpu.VMEM((2, rows // LANES, LANES), f32),
            pltpu.VMEM((GROUP, 1, shard), f32),
            pltpu.VMEM((2, GROUP, 8, shard), f32),
            pltpu.VMEM((rows // LANES, LANES), f32),
            pltpu.VMEM((2, 2, 2 * REPS, rows // LANES, LANES), f32),
            pltpu.VMEM((2, GROUP, 1, shard), f32),
            pltpu.VMEM((2, GROUP, 1, shard), f32),
            pltpu.SemaphoreType.DMA((5,)),
            pltpu.SemaphoreType.DMA((2,)),
            pltpu.SemaphoreType.DMA((2,)),
            pltpu.SemaphoreType.DMA((REPS,)),
            pltpu.SemaphoreType.DMA((1,)),
            pltpu.SemaphoreType.DMA((GROUP,)),
            pltpu.SemaphoreType.DMA((1,)),
            pltpu.SemaphoreType.DMA((2,)),
            pltpu.SemaphoreType.DMA((2, 2)),
            pltpu.SemaphoreType.DMA((2, 2)),
            pltpu.SemaphoreType.DMA((2,)),
            pltpu.SemaphoreType.DMA((2,)),
        ],
        compiler_params=pltpu.CompilerParams(
            collective_id=0, has_side_effects=True, vmem_limit_bytes=63 * 1024 * 1024
        ),
        name="sinkhorn",
    )(
        source,
        target,
        row_logw.reshape(rows // LANES, LANES),
        col_logw.reshape(1, shard),
        support,
    )
    return row_dual.reshape(rows), col_dual.reshape(shard)


def solution(mesh):
    placed = (P("tile", None), P(("rep", "tile"), None), P("tile"), P(("rep", "tile")), P())
    return jax.shard_map(
        per_device,
        mesh=mesh,
        in_specs=placed,
        out_specs=(P("tile"), P(("rep", "tile"))),
        check_vma=False,
    )
```

```python
import functools
import math

import jax
import jax.numpy as jnp
from jax import lax
from jax.experimental import pallas as pl
from jax.experimental.pallas import tpu as pltpu
from jax.sharding import PartitionSpec as P

MESH = pl.DeviceIdType.MESH
EPS = 0.1
NEG = -1e30
LOG2E = 1.0 / math.log(2.0)
LN2 = math.log(2.0)
NX = 4
TILES = 2 * NX * NX
GROUP = TILES // 2
REPS = 4
LANES = 128


def kernel(
    source_hbm,
    target_hbm,
    row_logw_hbm,
    col_logw_hbm,
    support_hbm,
    row_out,
    col_out,
    src,
    tgt,
    row_logw,
    col_logw,
    support,
    prod,
    stage_a,
    stage_b,
    m_run,
    s_run,
    b_col,
    b_keep,
    a_all,
    a_wide,
    row_sq,
    row_part,
    col_part,
    col_all,
    col_in,
    local_sem,
    logw_sem,
    src_send,
    src_recv,
    gather_send,
    gather_recv,
    all_send,
    all_recv,
    row_send,
    row_recv,
    col_send,
    col_recv,
):
    rows = src.shape[1]
    shard = col_logw.shape[1]
    depth = src.shape[2]
    blocks = TILES * shard // rows
    per_block = TILES // blocks
    chunks = rows // LANES
    halves = shard // LANES
    me = lax.axis_index("tile")
    rep = lax.axis_index("rep")
    core = me % 2
    x = me // (2 * NX)
    z = (me // 2) % NX
    half = x // 2
    xl = x % 2
    base = half * GROUP
    slot = me - base
    partner = me + 1 - 2 * core
    across = ((NX - 1 - x) * NX + z) * 2 + core
    row_tiles = [me * (1 - half) + across * half, across * (1 - half) + me * half]
    score_scale = 2.0 * LOG2E / (depth * EPS)
    square_scale = LOG2E / (depth * EPS)
    dual_scale = EPS * LN2

    zs = [(z + i) % NX for i in range(NX)]
    xls = [xl, 1 - xl]

    def place(dx, dz, of):
        return (xls[dx] * NX + zs[dz]) * 2 + of

    def mine(dx, dz):
        return place(dx, dz, core)

    def theirs(dx, dz):
        return place(dx, dz, 1 - core)

    def chip(step):
        m = NX - 1 - step % NX
        dz = m + m // 2 - 2 * (m // 3)
        return (((xl + 1 - step // NX) % 2) * NX + (z + dz) % NX) * 2

    def each_chip(visit):
        def one(step, at):
            visit(step, at)
            return chip(step + 1)

        lax.fori_loop(0, GROUP // 2 - 1, one, chip(0))

    def to_others(start):
        def both(step, at):
            start(2 * step, at + core)
            start(2 * step + 1, at + 1 - core)

        each_chip(both)
        start(GROUP - 2, slot + 1 - 2 * core)

    def reached(j, c):
        return (j + 16 - c) // 16

    def pair_at(p):
        turn = (p + 1) % 3
        dz = (1 + 2 * turn - 3 * (turn // 2)) * reached(p, 2)
        dx = reached(p, 1) - reached(p, 2) + reached(p, 5)
        return (((xl + dx) % 2) * NX + (z + dz) % NX) * 2

    row_peers = [{"tile": me, "rep": (rep + i) % REPS} for i in range(1, REPS)]
    row_peers += [{"tile": across, "rep": (rep + i) % REPS} for i in range(REPS)]

    loads = [
        pltpu.make_async_copy(target_hbm, tgt.at[slot, pl.ds(0, shard)], local_sem.at[0]),
        pltpu.make_async_copy(source_hbm, src.at[half], local_sem.at[1]),
        pltpu.make_async_copy(support_hbm, support, local_sem.at[2]),
        pltpu.make_async_copy(row_logw_hbm, row_logw.at[half], local_sem.at[3]),
        pltpu.make_async_copy(col_logw_hbm, col_logw, local_sem.at[4]),
    ]
    for load in loads:
        load.start()

    barrier = pltpu.get_barrier_semaphore()

    def greet(message, at):
        pl.semaphore_signal(
            barrier, inc=1, device_id={"tile": base + at}, device_id_type=MESH
        )

    to_others(greet)
    for peer in row_peers:
        pl.semaphore_signal(barrier, inc=1, device_id=peer, device_id_type=MESH)

    loads[0].wait()
    loads[4].wait()
    own = tgt[slot, :shard].astype(jnp.float32)
    own_sq = jnp.sum((own * own).T, axis=0, keepdims=True)
    parts = []
    for rest in (-square_scale * own_sq, col_logw[...]):
        for _ in range(3):
            parts.append(rest.astype(jnp.bfloat16))
            rest = rest - parts[-1].astype(jnp.float32)
    extra = tgt.shape[1] - shard
    tgt[slot, shard:] = jnp.concatenate(
        parts + [jnp.zeros((extra - 6, depth), jnp.bfloat16)], axis=0
    )

    pl.semaphore_wait(barrier, GROUP - 1 + len(row_peers))

    quarter = rows // REPS

    def rows_at(i):
        return pl.ds(pl.multiple_of((rep + i) % REPS * quarter, quarter), quarter)

    def send_rows(i, sem):
        pltpu.make_async_remote_copy(
            src_ref=source_hbm.at[rows_at(i)],
            dst_ref=src.at[half, rows_at(i)],
            send_sem=src_send.at[sem],
            recv_sem=src_recv.at[(rep + i) % REPS],
            device_id={"tile": across},
            device_id_type=MESH,
        ).start()

    def wait_rows(i):
        view = src.at[1 - half, rows_at(i)]
        pltpu.make_async_copy(view, view, src_recv.at[(rep + i) % REPS]).wait()

    def pass_rows(to):
        view = src.at[1 - half, rows_at(0)]
        pltpu.make_async_remote_copy(
            src_ref=view,
            dst_ref=view,
            send_sem=src_send.at[1],
            recv_sem=src_recv.at[rep],
            device_id={"rep": (rep + to) % REPS},
            device_id_type=MESH,
        ).start()

    def send_shard(k, to):
        pltpu.make_async_remote_copy(
            src_ref=tgt.at[k],
            dst_ref=tgt.at[k],
            send_sem=gather_send.at[0],
            recv_sem=gather_recv.at[k],
            device_id={"tile": base + to},
            device_id_type=MESH,
        ).start()

    def wait_shard(k):
        pltpu.make_async_copy(tgt.at[k], tgt.at[k], gather_recv.at[k]).wait()

    partner_slot = slot + 1 - 2 * core
    send_rows(0, 0)
    send_shard(slot, mine(1, 0))
    for dz in (1, 3):
        send_shard(slot, mine(0, dz))
    send_shard(slot, partner_slot)
    logw_copy = pltpu.make_async_remote_copy(
        src_ref=row_logw_hbm,
        dst_ref=row_logw.at[half],
        send_sem=logw_sem.at[0],
        recv_sem=logw_sem.at[1],
        device_id={"tile": across},
        device_id_type=MESH,
    )
    logw_copy.start()

    def bias_of(i, k):
        tile = row_tiles[0] * (1 - i) + row_tiles[1] * i
        live = support[tile, rep * blocks + (base + k) // per_block]
        return (1.0 - live.astype(jnp.float32)) * NEG

    for load in loads[1:4]:
        load.wait()

    m_run[...] = jnp.full(m_run.shape, NEG, jnp.float32)
    s_run[...] = jnp.zeros(s_run.shape, jnp.float32)
    for q in range(chunks):
        cells = src[half, q * LANES : (q + 1) * LANES, :].astype(jnp.float32)
        sq = cells * cells
        sq = sum(sq[:, i * LANES : (i + 1) * LANES] for i in range(depth // LANES))
        row_sq[q : q + 1, :] = jnp.sum(sq.T, axis=0, keepdims=True)

    view = src.at[0, pl.ds(0, quarter)]
    pltpu.make_async_copy(view, view, src_send.at[0]).wait()
    send_rows(2, 1)
    send_shard(slot, mine(0, 2))

    def against(left, right):
        return lax.dot_general(
            left, right, (((1,), (1,)), ((), ())), preferred_element_type=jnp.float32
        )

    def products(i, pair, stage):
        for n, k in enumerate(pair):
            for r in range(0, rows, 512):
                stage[n, r : r + 512, :] = against(src[i, r : r + 512, :], tgt[k, :shard])

    def column_term(k):
        parts = tgt[k, shard:].astype(jnp.float32)
        return parts[0:1] + parts[1:2] + parts[2:3]

    def update(i, pair, stage, terms):
        step = 32
        for r in range(0, rows, step):
            at = slice(r, r + step)
            t = []
            for n, k in enumerate(pair):
                p = stage[n, at, :] * score_scale
                prod[k, i, at, :] = p
                t.extend(
                    p[:, h * LANES : (h + 1) * LANES] + terms[n][:, h * LANES : (h + 1) * LANES]
                    for h in range(halves)
                )
            old = m_run[i, at, :]
            new = functools.reduce(jnp.maximum, t, old)
            m_run[i, at, :] = new
            s_run[i, at, :] = s_run[i, at, :] * jnp.exp2(old - new) + sum(
                jnp.exp2(v - new) for v in t
            )

    def receive(p):
        k = pair_at(p) + core
        wait_shard(k)

        @pl.when(core * 8 + p == 1)
        def _():
            for dz in (1, 3, 2):
                send_shard(k, mine(0, dz))

        @pl.when(core * reached(p, 2) * (1 - reached(p, 5)) == 1)
        def _():
            send_shard(k, mine(1, 0))

        send_shard(k, partner_slot)

    def receive_theirs(p):
        wait_shard(pair_at(p) + 1 - core)

    def rows_of(other):
        return half + other * (1 - 2 * half)

    def step_at(n):
        a, b, c = reached(n, 5), reached(n, 10), reached(n, 13)
        at = pair_at(n - 5 * a - 3 * c)
        return half * (1 - a) + (1 - half) * (a - b) + c, at

    row_slot = half * REPS + rep

    def send_row_sums(iteration, block):
        for peer in row_peers:
            pltpu.make_async_remote_copy(
                src_ref=row_part.at[iteration, block, row_slot],
                dst_ref=row_part.at[iteration, block, row_slot],
                send_sem=row_send.at[iteration, block],
                recv_sem=row_recv.at[iteration, block],
                device_id=peer,
                device_id_type=MESH,
            ).start()

    def take_row_sums(iteration, block):
        view = row_part.at[iteration, block, pl.ds(0, len(row_peers))]
        pltpu.make_async_copy(view, view, row_recv.at[iteration, block]).wait()
        return [row_part[iteration, block, i] for i in range(2 * REPS)]

    def spread_rows(block, values):
        for q in range(chunks):
            b_col[block, q * LANES : (q + 1) * LANES, :] = jnp.broadcast_to(
                values[q : q + 1, :], (LANES, LANES)
            ).T

    def fold_log_rows(block):
        for q in range(chunks):
            at = slice(q * LANES, (q + 1) * LANES)
            m = m_run[block, at, :].T
            s = s_run[block, at, :].T
            peak = jnp.max(m, axis=0, keepdims=True)
            total = jnp.sum(s * jnp.exp2(m - peak), axis=0, keepdims=True)
            row_part[0, block, row_slot, q : q + 1, :] = peak + jnp.log2(total)
        send_row_sums(0, block)

    def multiply(now, stage):
        i, at = now
        products(i, (at, at + 1), stage)

    def fold_in(now, stage, terms):
        i, at = now
        update(i, (at, at + 1), stage, terms)

    def terms_of(now):
        i, at = now
        bias = bias_of(i, at)
        return [column_term(k) + bias for k in (at, at + 1)]

    now = step_at(0)
    receive_theirs(0)
    multiply(now, stage_a)
    fold_in(now, stage_a, terms_of(now))
    receive(1)
    wait_rows(0)
    pass_rows(1)
    pass_rows(3)
    receive_theirs(1)
    multiply(step_at(1), stage_a)

    def turn(j, carry):
        @pl.when(j == 6)
        def _():
            fold_log_rows(0)

        now, later, last = carry

        @pl.when(j == 0)
        def _():
            receive(2)
            receive(3)
            receive_theirs(2)

        @pl.when(j == 1)
        def _():
            receive(4)
            receive_theirs(4)

        @pl.when(j == 2)
        def _():
            receive(5)

        @pl.when(j == 3)
        def _():
            receive(7)

        @pl.when(j == 4)
        def _():
            receive_theirs(5)

        @pl.when(j == 5)
        def _():
            receive_theirs(7)

        terms = terms_of(now)
        multiply(later, stage_b)
        fold_in(now, stage_a, terms)

        @pl.when(j == 0)
        def _():
            receive_theirs(3)

        @pl.when(j == 1)
        def _():
            for i in (2, 1, 3):
                wait_rows(i)

        @pl.when(j == 2)
        def _():
            receive(6)

        @pl.when(j == 4)
        def _():
            receive_theirs(6)

        terms = terms_of(later)
        multiply(last, stage_a)
        fold_in(later, stage_b, terms)
        return last, step_at(2 * j + 4), step_at(2 * j + 5)

    now, _, _ = lax.fori_loop(0, 7, turn, (step_at(1), step_at(2), step_at(3)))
    fold_in(now, stage_a, terms_of(now))
    fold_log_rows(1)
    logw_copy.wait()

    def finish_log_rows(block):
        parts = take_row_sums(0, block)
        peak = functools.reduce(jnp.maximum, parts)
        total = sum(jnp.exp2(v - peak) for v in parts)
        b = LOG2E * row_logw[block] - (peak + jnp.log2(total))
        b_keep[block] = b
        spread_rows(block, b)

    groups = LANES // 8

    def tree(op, v):
        while v.shape[0] > 1:
            n = v.shape[0] // 2
            v = op(v[:n], v[n:])
        return v[0]

    def lane_tiles(v):
        return [v[..., i * LANES : (i + 1) * LANES] for i in range(halves)]

    def tiles_of(pair):
        return [(k, slice(i * LANES, (i + 1) * LANES)) for k in pair for i in range(halves)]

    def log_columns(pair, block):
        tiles = tiles_of(pair)
        biases = [bias_of(block, k) for k in pair]
        peaks = [jnp.full((8, LANES), NEG, jnp.float32)] * len(tiles)
        totals = [jnp.zeros((8, LANES), jnp.float32)] * len(tiles)
        for q in range(chunks):
            at = slice(q * LANES, (q + 1) * LANES)
            row_term = b_col[block, at, :]
            for n, (k, lanes) in enumerate(tiles):
                t = prod[k, block, at, lanes] + row_term
                prod[k, block, at, lanes] = t
                t = t.reshape(groups, 8, LANES)
                new = jnp.maximum(peaks[n], tree(jnp.maximum, t))
                totals[n] = totals[n] * jnp.exp2(peaks[n] - new) + tree(
                    jnp.add, jnp.exp2(t - new[None])
                )
                peaks[n] = new
        parts = []
        for n in range(len(tiles)):
            top = jnp.max(peaks[n], axis=0, keepdims=True)
            total = jnp.sum(totals[n] * jnp.exp2(peaks[n] - top), axis=0, keepdims=True)
            parts.append(top + jnp.log2(total) + biases[n // halves])
        return parts

    def log_first(pair):
        for (k, lanes), part in zip(tiles_of(pair), log_columns(pair, 0)):
            col_part[0, k, :, lanes] = part

    def log_second(pair):
        for (k, lanes), two in zip(tiles_of(pair), log_columns(pair, 1)):
            one = col_part[0, k, :, lanes]
            top = jnp.maximum(one, two)
            col_part[0, k, :, lanes] = top + jnp.log2(jnp.exp2(one - top) + jnp.exp2(two - top))

    def sum_columns(pair, block):
        tiles = tiles_of(pair)

        def some(q, carry):
            at = pl.ds(pl.multiple_of(q * LANES, LANES), LANES)
            row_term = b_col[block, at, :]
            out = []
            for (k, lanes), total in zip(tiles, carry):
                t = (prod[k, block, at, lanes] * row_term).reshape(4, 4, 8, LANES)
                out.append(total + ((t[0] + t[1]) + (t[2] + t[3])))
            return tuple(out)

        start = (jnp.zeros((4, 8, LANES), jnp.float32),) * len(tiles)
        totals = lax.fori_loop(0, chunks, some, start, unroll=2)
        return [jnp.sum(tree(jnp.add, total), axis=0, keepdims=True) for total in totals]

    def sum_first(pair):
        for (k, lanes), part in zip(tiles_of(pair), sum_columns(pair, 0)):
            col_part[1, k, :, lanes] = part

    def sum_second(pair):
        for (k, lanes), part in zip(tiles_of(pair), sum_columns(pair, 1)):
            col_part[1, k, :, lanes] = col_part[1, k, :, lanes] + part

    def all_chips(visit):
        def one(n, carry):
            visit((2 * n, 2 * n + 1))
            return carry

        lax.fori_loop(0, GROUP // 2, one, 0)

    def column_pass(visit):
        def start(message, k):
            pltpu.make_async_remote_copy(
                src_ref=col_part.at[1, k],
                dst_ref=col_in.at[message],
                send_sem=col_send.at[0],
                recv_sem=col_recv.at[0],
                device_id={"tile": base + k},
                device_id_type=MESH,
            ).start()

        def both(step, at):
            visit((at, at + 1))
            start(2 * step, at + core)
            start(2 * step + 1, at + 1 - core)

        each_chip(both)
        visit((slot - core, slot - core + 1))
        start(GROUP - 2, partner_slot)
        col_in[GROUP - 1] = col_part[1, slot]
        view = col_in.at[pl.ds(0, GROUP - 1)]
        pltpu.make_async_copy(view, view, col_recv.at[0]).wait()
        return col_in[...]

    finish_log_rows(0)
    all_chips(log_first)
    finish_log_rows(1)
    groups_of_chips = ((0, 4), (4, 6), (6, 8))

    def share_columns(g):
        begin, end = groups_of_chips[g]
        these = pl.ds(2 * begin, 2 * (end - begin))
        col_all[slot, these] = col_part[0, these]

        def start(message, to):
            pltpu.make_async_remote_copy(
                src_ref=col_part.at[0, these],
                dst_ref=col_all.at[slot, these],
                send_sem=all_send.at[g],
                recv_sem=all_recv.at[g],
                device_id={"tile": base + to},
                device_id_type=MESH,
            ).start()

        to_others(start)

    def wait_columns(g, sem):
        begin, end = groups_of_chips[g]
        view = col_all.at[pl.ds(0, GROUP - 1), pl.ds(2 * begin, 2 * (end - begin))]
        pltpu.make_async_copy(view, view, sem).wait()

    def take_columns(g):
        wait_columns(g, all_recv.at[g])
        begin, end = groups_of_chips[g]
        for k in range(2 * begin, 2 * end):
            parts = [col_all[i, k] for i in range(GROUP)]
            peak = functools.reduce(jnp.maximum, parts)
            total = sum(jnp.exp2(v - peak) for v in parts)
            weights = tgt[k, shard:].astype(jnp.float32)
            weights = weights[3:4] + weights[4:5] + weights[5:6]
            a = LOG2E * weights - (peak + jnp.log2(total))
            a_all[k] = a
            for i in range(2):
                a_wide[i, k] = jnp.broadcast_to(a + bias_of(i, k), (8, shard))

    for g, (begin, end) in enumerate(groups_of_chips):

        def one(n, carry):
            log_second((2 * n, 2 * n + 1))
            return carry

        lax.fori_loop(begin, end, one, 0)
        share_columns(g)

    step_rows = 128

    def plan_rows(block, chips, more):
        slots = range(2 * chips[0], 2 * chips[1])

        def some(step, carry):
            at = pl.ds(pl.multiple_of(step * step_rows, step_rows), step_rows)
            totals = [jnp.zeros((step_rows // 8, 8, LANES), jnp.float32)] * 2
            if more:
                totals[0] = s_run[block, at, :].reshape(step_rows // 8, 8, LANES)
            for n, k in enumerate(slots):
                t = jnp.exp2(
                    prod[k, block, at, :].reshape(step_rows // 8, 8, shard)
                    + a_wide[block, k][None]
                )
                prod[k, block, at, :] = t.reshape(step_rows, shard)
                totals[n % 2] = totals[n % 2] + sum(lane_tiles(t))
            s_run[block, at, :] = sum(totals).reshape(step_rows, LANES)
            return carry

        lax.fori_loop(0, rows // step_rows, some, 0)

    def fold_rows(block):
        for q in range(chunks):
            at = slice(q * LANES, (q + 1) * LANES)
            row_part[1, block, row_slot, q : q + 1, :] = jnp.sum(
                s_run[block, at, :].T, axis=0, keepdims=True
            )
        send_row_sums(1, block)

    def finish_rows(block):
        total = sum(take_row_sums(1, block))
        spread_rows(block, jnp.exp2(LOG2E * row_logw[block]) / total)
        b_keep[block] = b_keep[block] + LOG2E * row_logw[block] - jnp.log2(total)

    for g, chips in enumerate(groups_of_chips):
        take_columns(g)
        plan_rows(0, chips, g > 0)
    fold_rows(0)
    plan_rows(1, (0, 8), False)
    fold_rows(1)
    finish_rows(0)
    all_chips(sum_first)
    finish_rows(1)

    total = jnp.sum(column_pass(sum_second), axis=0)
    a = a_all[slot] + LOG2E * col_logw[...] - jnp.log2(total)

    row_out[...] = row_sq[...] / depth + dual_scale * b_keep[half]
    col_out[...] = own_sq / depth + dual_scale * a

    view = tgt.at[pl.ds(0, GROUP - 1)]
    pltpu.make_async_copy(view, view, gather_send.at[0]).wait()
    view = src.at[0, pl.ds(0, 3 * quarter)]
    pltpu.make_async_copy(view, view, src_send.at[1]).wait()
    for g in range(len(groups_of_chips)):
        wait_columns(g, all_send.at[g])
    for iteration in range(2):
        for block in range(2):
            view = row_part.at[iteration, block, pl.ds(0, len(row_peers))]
            pltpu.make_async_copy(view, view, row_send.at[iteration, block]).wait()
    view = col_in.at[pl.ds(0, GROUP - 1)]
    pltpu.make_async_copy(view, view, col_send.at[0]).wait()


def per_device(source, target, row_logw, col_logw, support):
    rows, depth = source.shape
    shard = target.shape[0]
    vmem = pl.BlockSpec(memory_space=pltpu.VMEM)
    f32 = jnp.float32
    row_dual, col_dual = pl.pallas_call(
        kernel,
        out_shape=(
            jax.ShapeDtypeStruct((rows // LANES, LANES), f32),
            jax.ShapeDtypeStruct((1, shard), f32),
        ),
        in_specs=[pl.BlockSpec(memory_space=pl.ANY)] * 5,
        out_specs=(vmem, vmem),
        scratch_shapes=[
            pltpu.VMEM((2, rows, depth), source.dtype),
            pltpu.VMEM((GROUP, shard + 16, depth), target.dtype),
            pltpu.VMEM((2, rows // LANES, LANES), f32),
            pltpu.VMEM((1, shard), f32),
            pltpu.SMEM(support.shape, support.dtype),
            pltpu.VMEM((GROUP, 2, rows, shard), f32),
            pltpu.VMEM((2, rows, shard), f32),
            pltpu.VMEM((2, rows, shard), f32),
            pltpu.VMEM((2, rows, LANES), f32),
            pltpu.VMEM((2, rows, LANES), f32),
            pltpu.VMEM((2, rows, LANES), f32),
            pltpu.VMEM((2, rows // LANES, LANES), f32),
            pltpu.VMEM((GROUP, 1, shard), f32),
            pltpu.VMEM((2, GROUP, 8, shard), f32),
            pltpu.VMEM((rows // LANES, LANES), f32),
            pltpu.VMEM((2, 2, 2 * REPS, rows // LANES, LANES), f32),
            pltpu.VMEM((2, GROUP, 1, shard), f32),
            pltpu.VMEM((GROUP, GROUP, 1, shard), f32),
            pltpu.VMEM((GROUP, 1, shard), f32),
            pltpu.SemaphoreType.DMA((5,)),
            pltpu.SemaphoreType.DMA((2,)),
            pltpu.SemaphoreType.DMA((2,)),
            pltpu.SemaphoreType.DMA((REPS,)),
            pltpu.SemaphoreType.DMA((1,)),
            pltpu.SemaphoreType.DMA((GROUP,)),
            pltpu.SemaphoreType.DMA((3,)),
            pltpu.SemaphoreType.DMA((3,)),
            pltpu.SemaphoreType.DMA((2, 2)),
            pltpu.SemaphoreType.DMA((2, 2)),
            pltpu.SemaphoreType.DMA((1,)),
            pltpu.SemaphoreType.DMA((1,)),
        ],
        compiler_params=pltpu.CompilerParams(
            collective_id=0, has_side_effects=True, vmem_limit_bytes=63 * 1024 * 1024
        ),
        name="sinkhorn",
    )(
        source,
        target,
        row_logw.reshape(rows // LANES, LANES),
        col_logw.reshape(1, shard),
        support,
    )
    return row_dual.reshape(rows), col_dual.reshape(shard)


def solution(mesh):
    placed = (P("tile", None), P(("rep", "tile"), None), P("tile"), P(("rep", "tile")), P())
    return jax.shard_map(
        per_device,
        mesh=mesh,
        in_specs=placed,
        out_specs=(P("tile"), P(("rep", "tile"))),
        check_vma=False,
    )
```

```python
import functools
import math

import jax
import jax.numpy as jnp
from jax import lax
from jax.experimental import pallas as pl
from jax.experimental.pallas import tpu as pltpu
from jax.sharding import PartitionSpec as P

MESH = pl.DeviceIdType.MESH
EPS = 0.1
NEG = -1e30
LOG2E = 1.0 / math.log(2.0)
LN2 = math.log(2.0)
NX = 4
TILES = 2 * NX * NX
GROUP = TILES // 2
REPS = 4
LANES = 128


def kernel(
    source_hbm,
    target_hbm,
    row_logw_hbm,
    col_logw_hbm,
    support_hbm,
    row_out,
    col_out,
    src,
    tgt,
    row_logw,
    col_logw,
    support,
    prod,
    stage_a,
    stage_b,
    m_run,
    s_run,
    b_col,
    b_keep,
    a_all,
    a_wide,
    row_sq,
    row_part,
    col_part,
    col_all,
    col_in,
    local_sem,
    logw_sem,
    src_send,
    src_recv,
    gather_send,
    gather_recv,
    all_send,
    all_recv,
    row_send,
    row_recv,
    col_send,
    col_recv,
):
    rows = src.shape[1]
    shard = col_logw.shape[1]
    depth = src.shape[2]
    blocks = TILES * shard // rows
    per_block = TILES // blocks
    chunks = rows // LANES
    halves = shard // LANES
    me = lax.axis_index("tile")
    rep = lax.axis_index("rep")
    core = me % 2
    x = me // (2 * NX)
    z = (me // 2) % NX
    half = x // 2
    xl = x % 2
    base = half * GROUP
    slot = me - base
    partner = me + 1 - 2 * core
    across = ((NX - 1 - x) * NX + z) * 2 + core
    row_tiles = [me * (1 - half) + across * half, across * (1 - half) + me * half]
    score_scale = 2.0 * LOG2E / (depth * EPS)
    square_scale = LOG2E / (depth * EPS)
    dual_scale = EPS * LN2

    zs = [(z + i) % NX for i in range(NX)]
    xls = [xl, 1 - xl]

    def place(dx, dz, of):
        return (xls[dx] * NX + zs[dz]) * 2 + of

    def mine(dx, dz):
        return place(dx, dz, core)

    def theirs(dx, dz):
        return place(dx, dz, 1 - core)

    def chip(step):
        m = NX - 1 - step % NX
        dz = m + m // 2 - 2 * (m // 3)
        return (((xl + 1 - step // NX) % 2) * NX + (z + dz) % NX) * 2

    def each_chip(visit):
        def one(step, at):
            visit(step, at)
            return chip(step + 1)

        lax.fori_loop(0, GROUP // 2 - 1, one, chip(0))

    def to_others(start):
        def both(step, at):
            start(2 * step, at + core)
            start(2 * step + 1, at + 1 - core)

        each_chip(both)
        start(GROUP - 2, slot + 1 - 2 * core)

    def reached(j, c):
        return (j + 16 - c) // 16

    def pair_at(p):
        turn = (p + 1) % 3
        dz = (1 + 2 * turn - 3 * (turn // 2)) * reached(p, 2)
        dx = reached(p, 1) - reached(p, 2) + reached(p, 5)
        return (((xl + dx) % 2) * NX + (z + dz) % NX) * 2

    row_peers = [{"tile": me, "rep": (rep + i) % REPS} for i in range(1, REPS)]
    row_peers += [{"tile": across, "rep": (rep + i) % REPS} for i in range(REPS)]

    loads = [
        pltpu.make_async_copy(target_hbm, tgt.at[slot, pl.ds(0, shard)], local_sem.at[0]),
        pltpu.make_async_copy(source_hbm, src.at[half], local_sem.at[1]),
        pltpu.make_async_copy(support_hbm, support, local_sem.at[2]),
        pltpu.make_async_copy(row_logw_hbm, row_logw.at[half], local_sem.at[3]),
        pltpu.make_async_copy(col_logw_hbm, col_logw, local_sem.at[4]),
    ]
    for load in loads:
        load.start()

    barrier = pltpu.get_barrier_semaphore()

    def greet(message, at):
        pl.semaphore_signal(
            barrier, inc=1, device_id={"tile": base + at}, device_id_type=MESH
        )

    to_others(greet)
    for peer in row_peers:
        pl.semaphore_signal(barrier, inc=1, device_id=peer, device_id_type=MESH)

    loads[0].wait()
    loads[4].wait()
    own = tgt[slot, :shard].astype(jnp.float32)
    own_sq = jnp.sum((own * own).T, axis=0, keepdims=True)
    parts = []
    for rest in (-square_scale * own_sq, col_logw[...]):
        for _ in range(3):
            parts.append(rest.astype(jnp.bfloat16))
            rest = rest - parts[-1].astype(jnp.float32)
    extra = tgt.shape[1] - shard
    tgt[slot, shard:] = jnp.concatenate(
        parts + [jnp.zeros((extra - 6, depth), jnp.bfloat16)], axis=0
    )

    pl.semaphore_wait(barrier, GROUP - 1 + len(row_peers))

    quarter = rows // REPS

    def rows_at(i):
        return pl.ds(pl.multiple_of((rep + i) % REPS * quarter, quarter), quarter)

    def send_rows(i, sem):
        pltpu.make_async_remote_copy(
            src_ref=source_hbm.at[rows_at(i)],
            dst_ref=src.at[half, rows_at(i)],
            send_sem=src_send.at[sem],
            recv_sem=src_recv.at[(rep + i) % REPS],
            device_id={"tile": across},
            device_id_type=MESH,
        ).start()

    def wait_rows(i):
        view = src.at[1 - half, rows_at(i)]
        pltpu.make_async_copy(view, view, src_recv.at[(rep + i) % REPS]).wait()

    def pass_rows(to):
        view = src.at[1 - half, rows_at(0)]
        pltpu.make_async_remote_copy(
            src_ref=view,
            dst_ref=view,
            send_sem=src_send.at[1],
            recv_sem=src_recv.at[rep],
            device_id={"rep": (rep + to) % REPS},
            device_id_type=MESH,
        ).start()

    def send_shard(k, to):
        pltpu.make_async_remote_copy(
            src_ref=tgt.at[k],
            dst_ref=tgt.at[k],
            send_sem=gather_send.at[0],
            recv_sem=gather_recv.at[k],
            device_id={"tile": base + to},
            device_id_type=MESH,
        ).start()

    def wait_shard(k):
        pltpu.make_async_copy(tgt.at[k], tgt.at[k], gather_recv.at[k]).wait()

    partner_slot = slot + 1 - 2 * core
    send_rows(0, 0)
    send_shard(slot, mine(1, 0))
    for dz in (1, 3):
        send_shard(slot, mine(0, dz))
    send_shard(slot, partner_slot)
    logw_copy = pltpu.make_async_remote_copy(
        src_ref=row_logw_hbm,
        dst_ref=row_logw.at[half],
        send_sem=logw_sem.at[0],
        recv_sem=logw_sem.at[1],
        device_id={"tile": across},
        device_id_type=MESH,
    )
    logw_copy.start()

    def bias_of(i, k):
        tile = row_tiles[0] * (1 - i) + row_tiles[1] * i
        live = support[tile, rep * blocks + (base + k) // per_block]
        return (1.0 - live.astype(jnp.float32)) * NEG

    for load in loads[1:4]:
        load.wait()

    m_run[...] = jnp.full(m_run.shape, NEG, jnp.float32)
    s_run[...] = jnp.zeros(s_run.shape, jnp.float32)
    for q in range(chunks):
        cells = src[half, q * LANES : (q + 1) * LANES, :].astype(jnp.float32)
        sq = cells * cells
        sq = sum(sq[:, i * LANES : (i + 1) * LANES] for i in range(depth // LANES))
        row_sq[q : q + 1, :] = jnp.sum(sq.T, axis=0, keepdims=True)

    view = src.at[0, pl.ds(0, quarter)]
    pltpu.make_async_copy(view, view, src_send.at[0]).wait()
    send_rows(2, 1)
    send_shard(slot, mine(0, 2))

    def against(left, right):
        return lax.dot_general(
            left, right, (((1,), (1,)), ((), ())), preferred_element_type=jnp.float32
        )

    def products(i, pair, stage):
        for n, k in enumerate(pair):
            for r in range(0, rows, 512):
                stage[n, r : r + 512, :] = against(src[i, r : r + 512, :], tgt[k, :shard])

    def column_term(k):
        parts = tgt[k, shard:].astype(jnp.float32)
        return parts[0:1] + parts[1:2] + parts[2:3]

    def update(i, pair, stage, terms):
        step = 32
        for r in range(0, rows, step):
            at = slice(r, r + step)
            t = []
            for n, k in enumerate(pair):
                p = stage[n, at, :] * score_scale
                prod[k, i, at, :] = p
                t.extend(
                    p[:, h * LANES : (h + 1) * LANES] + terms[n][:, h * LANES : (h + 1) * LANES]
                    for h in range(halves)
                )
            old = m_run[i, at, :]
            new = functools.reduce(jnp.maximum, t, old)
            m_run[i, at, :] = new
            s_run[i, at, :] = s_run[i, at, :] * jnp.exp2(old - new) + sum(
                jnp.exp2(v - new) for v in t
            )

    def receive(p):
        k = pair_at(p) + core
        wait_shard(k)
        send_shard(k, partner_slot)

        @pl.when(core * 8 + p == 1)
        def _():
            for dz in (1, 3, 2):
                send_shard(k, mine(0, dz))

        @pl.when(core * reached(p, 2) * (1 - reached(p, 5)) == 1)
        def _():
            send_shard(k, mine(1, 0))

    def receive_theirs(p):
        wait_shard(pair_at(p) + 1 - core)

    def rows_of(other):
        return half + other * (1 - 2 * half)

    def step_at(n):
        a, b, c = reached(n, 5), reached(n, 10), reached(n, 13)
        at = pair_at(n - 5 * a - 3 * c)
        return half * (1 - a) + (1 - half) * (a - b) + c, at

    row_slot = half * REPS + rep

    def send_row_sums(iteration, block):
        for peer in row_peers:
            pltpu.make_async_remote_copy(
                src_ref=row_part.at[iteration, block, row_slot],
                dst_ref=row_part.at[iteration, block, row_slot],
                send_sem=row_send.at[iteration, block],
                recv_sem=row_recv.at[iteration, block],
                device_id=peer,
                device_id_type=MESH,
            ).start()

    def take_row_sums(iteration, block):
        view = row_part.at[iteration, block, pl.ds(0, len(row_peers))]
        pltpu.make_async_copy(view, view, row_recv.at[iteration, block]).wait()
        return [row_part[iteration, block, i] for i in range(2 * REPS)]

    def spread_rows(block, values):
        for q in range(chunks):
            b_col[block, q * LANES : (q + 1) * LANES, :] = jnp.broadcast_to(
                values[q : q + 1, :], (LANES, LANES)
            ).T

    def fold_log_rows(block):
        for q in range(chunks):
            at = slice(q * LANES, (q + 1) * LANES)
            m = m_run[block, at, :].T
            s = s_run[block, at, :].T
            peak = jnp.max(m, axis=0, keepdims=True)
            total = jnp.sum(s * jnp.exp2(m - peak), axis=0, keepdims=True)
            row_part[0, block, row_slot, q : q + 1, :] = peak + jnp.log2(total)
        send_row_sums(0, block)

    def multiply(now, stage):
        i, at = now
        products(i, (at, at + 1), stage)

    def fold_in(now, stage, terms):
        i, at = now
        update(i, (at, at + 1), stage, terms)

    def terms_of(now):
        i, at = now
        bias = bias_of(i, at)
        return [column_term(k) + bias for k in (at, at + 1)]

    now = step_at(0)
    receive_theirs(0)
    multiply(now, stage_a)
    fold_in(now, stage_a, terms_of(now))
    receive(1)
    wait_rows(0)
    pass_rows(1)
    pass_rows(3)
    receive_theirs(1)
    multiply(step_at(1), stage_a)

    def turn(j, carry):
        @pl.when(j == 6)
        def _():
            fold_log_rows(0)

        now, later, last = carry

        @pl.when(j == 0)
        def _():
            receive(2)
            receive(3)
            receive_theirs(2)

        @pl.when(j == 1)
        def _():
            receive(4)
            receive_theirs(4)

        @pl.when(j == 2)
        def _():
            receive(5)

        @pl.when(j == 3)
        def _():
            receive(7)

        @pl.when(j == 4)
        def _():
            receive_theirs(5)

        @pl.when(j == 5)
        def _():
            receive_theirs(7)

        terms = terms_of(now)
        multiply(later, stage_b)
        fold_in(now, stage_a, terms)

        @pl.when(j == 0)
        def _():
            receive_theirs(3)

        @pl.when(j == 1)
        def _():
            for i in (2, 1, 3):
                wait_rows(i)

        @pl.when(j == 2)
        def _():
            receive(6)

        @pl.when(j == 4)
        def _():
            receive_theirs(6)

        terms = terms_of(later)
        multiply(last, stage_a)
        fold_in(later, stage_b, terms)
        return last, step_at(2 * j + 4), step_at(2 * j + 5)

    now, _, _ = lax.fori_loop(0, 7, turn, (step_at(1), step_at(2), step_at(3)))
    fold_in(now, stage_a, terms_of(now))
    fold_log_rows(1)
    logw_copy.wait()

    def finish_log_rows(block):
        parts = take_row_sums(0, block)
        peak = functools.reduce(jnp.maximum, parts)
        total = sum(jnp.exp2(v - peak) for v in parts)
        b = LOG2E * row_logw[block] - (peak + jnp.log2(total))
        b_keep[block] = b
        spread_rows(block, b)

    groups = LANES // 8

    def tree(op, v):
        while v.shape[0] > 1:
            n = v.shape[0] // 2
            v = op(v[:n], v[n:])
        return v[0]

    def lane_tiles(v):
        return [v[..., i * LANES : (i + 1) * LANES] for i in range(halves)]

    def tiles_of(pair):
        return [(k, slice(i * LANES, (i + 1) * LANES)) for k in pair for i in range(halves)]

    def log_columns(pair, block):
        tiles = tiles_of(pair)
        biases = [bias_of(block, k) for k in pair]
        peaks = [jnp.full((8, LANES), NEG, jnp.float32)] * len(tiles)
        totals = [jnp.zeros((8, LANES), jnp.float32)] * len(tiles)
        for q in range(chunks):
            at = slice(q * LANES, (q + 1) * LANES)
            row_term = b_col[block, at, :]
            for n, (k, lanes) in enumerate(tiles):
                t = prod[k, block, at, lanes] + row_term
                prod[k, block, at, lanes] = t
                t = t.reshape(groups, 8, LANES)
                new = jnp.maximum(peaks[n], tree(jnp.maximum, t))
                totals[n] = totals[n] * jnp.exp2(peaks[n] - new) + tree(
                    jnp.add, jnp.exp2(t - new[None])
                )
                peaks[n] = new
        parts = []
        for n in range(len(tiles)):
            top = jnp.max(peaks[n], axis=0, keepdims=True)
            total = jnp.sum(totals[n] * jnp.exp2(peaks[n] - top), axis=0, keepdims=True)
            parts.append(top + jnp.log2(total) + biases[n // halves])
        return parts

    def log_first(pair):
        for (k, lanes), part in zip(tiles_of(pair), log_columns(pair, 0)):
            col_part[0, k, :, lanes] = part

    def log_second(pair):
        for (k, lanes), two in zip(tiles_of(pair), log_columns(pair, 1)):
            one = col_part[0, k, :, lanes]
            top = jnp.maximum(one, two)
            col_part[0, k, :, lanes] = top + jnp.log2(jnp.exp2(one - top) + jnp.exp2(two - top))

    def sum_columns(pair, block):
        tiles = tiles_of(pair)

        def some(q, carry):
            at = pl.ds(pl.multiple_of(q * LANES, LANES), LANES)
            row_term = b_col[block, at, :]
            out = []
            for (k, lanes), total in zip(tiles, carry):
                t = (prod[k, block, at, lanes] * row_term).reshape(4, 4, 8, LANES)
                out.append(total + ((t[0] + t[1]) + (t[2] + t[3])))
            return tuple(out)

        start = (jnp.zeros((4, 8, LANES), jnp.float32),) * len(tiles)
        totals = lax.fori_loop(0, chunks, some, start, unroll=2)
        return [jnp.sum(tree(jnp.add, total), axis=0, keepdims=True) for total in totals]

    def sum_first(pair):
        for (k, lanes), part in zip(tiles_of(pair), sum_columns(pair, 0)):
            col_part[1, k, :, lanes] = part

    def sum_second(pair):
        for (k, lanes), part in zip(tiles_of(pair), sum_columns(pair, 1)):
            col_part[1, k, :, lanes] = col_part[1, k, :, lanes] + part

    def all_chips(visit):
        def one(n, carry):
            visit((2 * n, 2 * n + 1))
            return carry

        lax.fori_loop(0, GROUP // 2, one, 0)

    def column_pass(visit):
        def start(message, k):
            pltpu.make_async_remote_copy(
                src_ref=col_part.at[1, k],
                dst_ref=col_in.at[message],
                send_sem=col_send.at[0],
                recv_sem=col_recv.at[0],
                device_id={"tile": base + k},
                device_id_type=MESH,
            ).start()

        def both(step, at):
            visit((at, at + 1))
            start(2 * step, at + core)
            start(2 * step + 1, at + 1 - core)

        each_chip(both)
        visit((slot - core, slot - core + 1))
        start(GROUP - 2, partner_slot)
        col_in[GROUP - 1] = col_part[1, slot]
        view = col_in.at[pl.ds(0, GROUP - 1)]
        pltpu.make_async_copy(view, view, col_recv.at[0]).wait()
        return col_in[...]

    finish_log_rows(0)
    all_chips(log_first)
    finish_log_rows(1)
    groups_of_chips = ((0, 4), (4, 6), (6, 8))

    def share_columns(g):
        begin, end = groups_of_chips[g]
        these = pl.ds(2 * begin, 2 * (end - begin))
        col_all[slot, these] = col_part[0, these]

        def start(message, to):
            pltpu.make_async_remote_copy(
                src_ref=col_part.at[0, these],
                dst_ref=col_all.at[slot, these],
                send_sem=all_send.at[g],
                recv_sem=all_recv.at[g],
                device_id={"tile": base + to},
                device_id_type=MESH,
            ).start()

        to_others(start)

    def wait_columns(g, sem):
        begin, end = groups_of_chips[g]
        view = col_all.at[pl.ds(0, GROUP - 1), pl.ds(2 * begin, 2 * (end - begin))]
        pltpu.make_async_copy(view, view, sem).wait()

    def take_columns(g):
        wait_columns(g, all_recv.at[g])
        begin, end = groups_of_chips[g]
        for k in range(2 * begin, 2 * end):
            parts = [col_all[i, k] for i in range(GROUP)]
            peak = functools.reduce(jnp.maximum, parts)
            total = sum(jnp.exp2(v - peak) for v in parts)
            weights = tgt[k, shard:].astype(jnp.float32)
            weights = weights[3:4] + weights[4:5] + weights[5:6]
            a = LOG2E * weights - (peak + jnp.log2(total))
            a_all[k] = a
            for i in range(2):
                a_wide[i, k] = jnp.broadcast_to(a + bias_of(i, k), (8, shard))

    for g, (begin, end) in enumerate(groups_of_chips):

        def one(n, carry):
            log_second((2 * n, 2 * n + 1))
            return carry

        lax.fori_loop(begin, end, one, 0)
        share_columns(g)

    step_rows = 128

    def plan_rows(block, chips, more):
        slots = range(2 * chips[0], 2 * chips[1])

        def some(step, carry):
            at = pl.ds(pl.multiple_of(step * step_rows, step_rows), step_rows)
            totals = [jnp.zeros((step_rows // 8, 8, LANES), jnp.float32)] * 2
            if more:
                totals[0] = s_run[block, at, :].reshape(step_rows // 8, 8, LANES)
            for n, k in enumerate(slots):
                t = jnp.exp2(
                    prod[k, block, at, :].reshape(step_rows // 8, 8, shard)
                    + a_wide[block, k][None]
                )
                prod[k, block, at, :] = t.reshape(step_rows, shard)
                totals[n % 2] = totals[n % 2] + sum(lane_tiles(t))
            s_run[block, at, :] = sum(totals).reshape(step_rows, LANES)
            return carry

        lax.fori_loop(0, rows // step_rows, some, 0)

    def fold_rows(block):
        for q in range(chunks):
            at = slice(q * LANES, (q + 1) * LANES)
            row_part[1, block, row_slot, q : q + 1, :] = jnp.sum(
                s_run[block, at, :].T, axis=0, keepdims=True
            )
        send_row_sums(1, block)

    def finish_rows(block):
        total = sum(take_row_sums(1, block))
        spread_rows(block, jnp.exp2(LOG2E * row_logw[block]) / total)
        b_keep[block] = b_keep[block] + LOG2E * row_logw[block] - jnp.log2(total)

    take_columns(0)
    plan_rows(0, (0, 4), False)
    take_columns(1)
    plan_rows(0, (4, 6), True)
    plan_rows(1, (0, 4), False)
    take_columns(2)
    plan_rows(0, (6, 8), True)
    fold_rows(0)
    plan_rows(1, (4, 8), True)
    fold_rows(1)
    finish_rows(0)
    all_chips(sum_first)
    finish_rows(1)

    total = jnp.sum(column_pass(sum_second), axis=0)
    a = a_all[slot] + LOG2E * col_logw[...] - jnp.log2(total)

    row_out[...] = row_sq[...] / depth + dual_scale * b_keep[half]
    col_out[...] = own_sq / depth + dual_scale * a

    view = tgt.at[pl.ds(0, GROUP - 1)]
    pltpu.make_async_copy(view, view, gather_send.at[0]).wait()
    view = src.at[0, pl.ds(0, 3 * quarter)]
    pltpu.make_async_copy(view, view, src_send.at[1]).wait()
    for g in range(len(groups_of_chips)):
        wait_columns(g, all_send.at[g])
    for iteration in range(2):
        for block in range(2):
            view = row_part.at[iteration, block, pl.ds(0, len(row_peers))]
            pltpu.make_async_copy(view, view, row_send.at[iteration, block]).wait()
    view = col_in.at[pl.ds(0, GROUP - 1)]
    pltpu.make_async_copy(view, view, col_send.at[0]).wait()


def per_device(source, target, row_logw, col_logw, support):
    rows, depth = source.shape
    shard = target.shape[0]
    vmem = pl.BlockSpec(memory_space=pltpu.VMEM)
    f32 = jnp.float32
    row_dual, col_dual = pl.pallas_call(
        kernel,
        out_shape=(
            jax.ShapeDtypeStruct((rows // LANES, LANES), f32),
            jax.ShapeDtypeStruct((1, shard), f32),
        ),
        in_specs=[pl.BlockSpec(memory_space=pl.ANY)] * 5,
        out_specs=(vmem, vmem),
        scratch_shapes=[
            pltpu.VMEM((2, rows, depth), source.dtype),
            pltpu.VMEM((GROUP, shard + 16, depth), target.dtype),
            pltpu.VMEM((2, rows // LANES, LANES), f32),
            pltpu.VMEM((1, shard), f32),
            pltpu.SMEM(support.shape, support.dtype),
            pltpu.VMEM((GROUP, 2, rows, shard), f32),
            pltpu.VMEM((2, rows, shard), f32),
            pltpu.VMEM((2, rows, shard), f32),
            pltpu.VMEM((2, rows, LANES), f32),
            pltpu.VMEM((2, rows, LANES), f32),
            pltpu.VMEM((2, rows, LANES), f32),
            pltpu.VMEM((2, rows // LANES, LANES), f32),
            pltpu.VMEM((GROUP, 1, shard), f32),
            pltpu.VMEM((2, GROUP, 8, shard), f32),
            pltpu.VMEM((rows // LANES, LANES), f32),
            pltpu.VMEM((2, 2, 2 * REPS, rows // LANES, LANES), f32),
            pltpu.VMEM((2, GROUP, 1, shard), f32),
            pltpu.VMEM((GROUP, GROUP, 1, shard), f32),
            pltpu.VMEM((GROUP, 1, shard), f32),
            pltpu.SemaphoreType.DMA((5,)),
            pltpu.SemaphoreType.DMA((2,)),
            pltpu.SemaphoreType.DMA((2,)),
            pltpu.SemaphoreType.DMA((REPS,)),
            pltpu.SemaphoreType.DMA((1,)),
            pltpu.SemaphoreType.DMA((GROUP,)),
            pltpu.SemaphoreType.DMA((3,)),
            pltpu.SemaphoreType.DMA((3,)),
            pltpu.SemaphoreType.DMA((2, 2)),
            pltpu.SemaphoreType.DMA((2, 2)),
            pltpu.SemaphoreType.DMA((1,)),
            pltpu.SemaphoreType.DMA((1,)),
        ],
        compiler_params=pltpu.CompilerParams(
            collective_id=0, has_side_effects=True, vmem_limit_bytes=63 * 1024 * 1024
        ),
        name="sinkhorn",
    )(
        source,
        target,
        row_logw.reshape(rows // LANES, LANES),
        col_logw.reshape(1, shard),
        support,
    )
    return row_dual.reshape(rows), col_dual.reshape(shard)


def solution(mesh):
    placed = (P("tile", None), P(("rep", "tile"), None), P("tile"), P(("rep", "tile")), P())
    return jax.shard_map(
        per_device,
        mesh=mesh,
        in_specs=placed,
        out_specs=(P("tile"), P(("rep", "tile"))),
        check_vma=False,
    )
```

```python
import functools
import math

import jax
import jax.numpy as jnp
from jax import lax
from jax.experimental import pallas as pl
from jax.experimental.pallas import tpu as pltpu
from jax.sharding import PartitionSpec as P

MESH = pl.DeviceIdType.MESH
EPS = 0.1
NEG = -1e30
LOG2E = 1.0 / math.log(2.0)
LN2 = math.log(2.0)
NX = 4
TILES = 2 * NX * NX
GROUP = TILES // 2
REPS = 4
LANES = 128


def kernel(
    source_hbm,
    target_hbm,
    row_logw_hbm,
    col_logw_hbm,
    support_hbm,
    row_out,
    col_out,
    src,
    tgt,
    row_logw,
    col_logw,
    support,
    prod,
    stage_a,
    stage_b,
    m_run,
    s_run,
    b_col,
    b_keep,
    a_all,
    a_wide,
    row_sq,
    row_part,
    col_part,
    col_all,
    col_in,
    local_sem,
    logw_sem,
    src_send,
    src_recv,
    gather_send,
    gather_recv,
    all_send,
    all_recv,
    row_send,
    row_recv,
    col_send,
    col_recv,
):
    rows = src.shape[1]
    shard = col_logw.shape[1]
    depth = src.shape[2]
    blocks = TILES * shard // rows
    per_block = TILES // blocks
    chunks = rows // LANES
    halves = shard // LANES
    me = lax.axis_index("tile")
    rep = lax.axis_index("rep")
    core = me % 2
    x = me // (2 * NX)
    z = (me // 2) % NX
    half = x // 2
    xl = x % 2
    base = half * GROUP
    slot = me - base
    partner = me + 1 - 2 * core
    across = ((NX - 1 - x) * NX + z) * 2 + core
    row_tiles = [me * (1 - half) + across * half, across * (1 - half) + me * half]
    score_scale = 2.0 * LOG2E / (depth * EPS)
    square_scale = LOG2E / (depth * EPS)
    dual_scale = EPS * LN2

    zs = [(z + i) % NX for i in range(NX)]
    xls = [xl, 1 - xl]

    def place(dx, dz, of):
        return (xls[dx] * NX + zs[dz]) * 2 + of

    def mine(dx, dz):
        return place(dx, dz, core)

    def theirs(dx, dz):
        return place(dx, dz, 1 - core)

    def chip(step):
        m = NX - 1 - step % NX
        dz = m + m // 2 - 2 * (m // 3)
        return (((xl + 1 - step // NX) % 2) * NX + (z + dz) % NX) * 2

    def each_chip(visit):
        def one(step, at):
            visit(step, at)
            return chip(step + 1)

        lax.fori_loop(0, GROUP // 2 - 1, one, chip(0))

    def to_others(start):
        def both(step, at):
            start(2 * step, at + core)
            start(2 * step + 1, at + 1 - core)

        each_chip(both)
        start(GROUP - 2, slot + 1 - 2 * core)

    def reached(j, c):
        return (j + 16 - c) // 16

    def pair_at(p):
        turn = (p + 1) % 3
        dz = (1 + 2 * turn - 3 * (turn // 2)) * reached(p, 2)
        dx = reached(p, 1) - reached(p, 2) + reached(p, 5)
        return (((xl + dx) % 2) * NX + (z + dz) % NX) * 2

    row_peers = [{"tile": me, "rep": (rep + i) % REPS} for i in range(1, REPS)]
    row_peers += [{"tile": across, "rep": (rep + i) % REPS} for i in range(REPS)]

    loads = [
        pltpu.make_async_copy(target_hbm, tgt.at[slot, pl.ds(0, shard)], local_sem.at[0]),
        pltpu.make_async_copy(source_hbm, src.at[half], local_sem.at[1]),
        pltpu.make_async_copy(support_hbm, support, local_sem.at[2]),
        pltpu.make_async_copy(row_logw_hbm, row_logw.at[half], local_sem.at[3]),
        pltpu.make_async_copy(col_logw_hbm, col_logw, local_sem.at[4]),
    ]
    for load in loads:
        load.start()

    barrier = pltpu.get_barrier_semaphore()

    def greet(message, at):
        pl.semaphore_signal(
            barrier, inc=1, device_id={"tile": base + at}, device_id_type=MESH
        )

    to_others(greet)
    for peer in row_peers:
        pl.semaphore_signal(barrier, inc=1, device_id=peer, device_id_type=MESH)

    loads[0].wait()
    loads[4].wait()
    own = tgt[slot, :shard].astype(jnp.float32)
    own_sq = jnp.sum((own * own).T, axis=0, keepdims=True)
    parts = []
    for rest in (-square_scale * own_sq, col_logw[...]):
        for _ in range(3):
            parts.append(rest.astype(jnp.bfloat16))
            rest = rest - parts[-1].astype(jnp.float32)
    extra = tgt.shape[1] - shard
    tgt[slot, shard:] = jnp.concatenate(
        parts + [jnp.zeros((extra - 6, depth), jnp.bfloat16)], axis=0
    )

    pl.semaphore_wait(barrier, GROUP - 1 + len(row_peers))

    quarter = rows // REPS

    def rows_at(i):
        return pl.ds(pl.multiple_of((rep + i) % REPS * quarter, quarter), quarter)

    def send_rows(i, sem):
        pltpu.make_async_remote_copy(
            src_ref=source_hbm.at[rows_at(i)],
            dst_ref=src.at[half, rows_at(i)],
            send_sem=src_send.at[sem],
            recv_sem=src_recv.at[(rep + i) % REPS],
            device_id={"tile": across},
            device_id_type=MESH,
        ).start()

    def wait_rows(i):
        view = src.at[1 - half, rows_at(i)]
        pltpu.make_async_copy(view, view, src_recv.at[(rep + i) % REPS]).wait()

    def pass_rows(to):
        view = src.at[1 - half, rows_at(0)]
        pltpu.make_async_remote_copy(
            src_ref=view,
            dst_ref=view,
            send_sem=src_send.at[1],
            recv_sem=src_recv.at[rep],
            device_id={"rep": (rep + to) % REPS},
            device_id_type=MESH,
        ).start()

    def send_shard(k, to):
        pltpu.make_async_remote_copy(
            src_ref=tgt.at[k],
            dst_ref=tgt.at[k],
            send_sem=gather_send.at[0],
            recv_sem=gather_recv.at[k],
            device_id={"tile": base + to},
            device_id_type=MESH,
        ).start()

    def wait_shard(k):
        pltpu.make_async_copy(tgt.at[k], tgt.at[k], gather_recv.at[k]).wait()

    partner_slot = slot + 1 - 2 * core
    send_rows(0, 0)
    send_shard(slot, mine(1, 0))
    for dz in (1, 3):
        send_shard(slot, mine(0, dz))
    send_shard(slot, partner_slot)
    logw_copy = pltpu.make_async_remote_copy(
        src_ref=row_logw_hbm,
        dst_ref=row_logw.at[half],
        send_sem=logw_sem.at[0],
        recv_sem=logw_sem.at[1],
        device_id={"tile": across},
        device_id_type=MESH,
    )
    logw_copy.start()

    def bias_of(i, k):
        tile = row_tiles[0] * (1 - i) + row_tiles[1] * i
        live = support[tile, rep * blocks + (base + k) // per_block]
        return (1.0 - live.astype(jnp.float32)) * NEG

    for load in loads[1:4]:
        load.wait()

    m_run[...] = jnp.full(m_run.shape, NEG, jnp.float32)
    s_run[...] = jnp.zeros(s_run.shape, jnp.float32)
    for q in range(chunks):
        cells = src[half, q * LANES : (q + 1) * LANES, :].astype(jnp.float32)
        sq = cells * cells
        sq = sum(sq[:, i * LANES : (i + 1) * LANES] for i in range(depth // LANES))
        row_sq[q : q + 1, :] = jnp.sum(sq.T, axis=0, keepdims=True)

    view = src.at[0, pl.ds(0, quarter)]
    pltpu.make_async_copy(view, view, src_send.at[0]).wait()
    send_rows(2, 1)
    send_shard(slot, mine(0, 2))

    def against(left, right):
        return lax.dot_general(
            left, right, (((1,), (1,)), ((), ())), preferred_element_type=jnp.float32
        )

    def products(i, pair, stage):
        for n, k in enumerate(pair):
            for r in range(0, rows, 512):
                stage[n, r : r + 512, :] = against(src[i, r : r + 512, :], tgt[k, :shard])

    def column_term(k):
        parts = tgt[k, shard:].astype(jnp.float32)
        return parts[0:1] + parts[1:2] + parts[2:3]

    def update(i, pair, stage, terms):
        step = 32
        for r in range(0, rows, step):
            at = slice(r, r + step)
            t = []
            for n, k in enumerate(pair):
                p = stage[n, at, :] * score_scale
                prod[k, i, at, :] = p
                t.extend(
                    p[:, h * LANES : (h + 1) * LANES] + terms[n][:, h * LANES : (h + 1) * LANES]
                    for h in range(halves)
                )
            old = m_run[i, at, :]
            new = functools.reduce(jnp.maximum, t, old)
            m_run[i, at, :] = new
            s_run[i, at, :] = s_run[i, at, :] * jnp.exp2(old - new) + sum(
                jnp.exp2(v - new) for v in t
            )

    def receive(p):
        k = pair_at(p) + core
        wait_shard(k)
        send_shard(k, partner_slot)

        @pl.when(core * 8 + p == 1)
        def _():
            for dz in (1, 3, 2):
                send_shard(k, mine(0, dz))

        @pl.when(core * reached(p, 2) * (1 - reached(p, 5)) == 1)
        def _():
            send_shard(k, mine(1, 0))

    def receive_theirs(p):
        wait_shard(pair_at(p) + 1 - core)

    def rows_of(other):
        return half + other * (1 - 2 * half)

    def step_at(n):
        a, b, c = reached(n, 5), reached(n, 10), reached(n, 13)
        at = pair_at(n - 5 * a - 3 * c)
        return half * (1 - a) + (1 - half) * (a - b) + c, at

    row_slot = half * REPS + rep

    def send_row_sums(iteration, block):
        for peer in row_peers:
            pltpu.make_async_remote_copy(
                src_ref=row_part.at[iteration, block, row_slot],
                dst_ref=row_part.at[iteration, block, row_slot],
                send_sem=row_send.at[iteration, block],
                recv_sem=row_recv.at[iteration, block],
                device_id=peer,
                device_id_type=MESH,
            ).start()

    def take_row_sums(iteration, block):
        view = row_part.at[iteration, block, pl.ds(0, len(row_peers))]
        pltpu.make_async_copy(view, view, row_recv.at[iteration, block]).wait()
        return [row_part[iteration, block, i] for i in range(2 * REPS)]

    def spread_rows(block, values):
        for q in range(chunks):
            b_col[block, q * LANES : (q + 1) * LANES, :] = jnp.broadcast_to(
                values[q : q + 1, :], (LANES, LANES)
            ).T

    def fold_log_rows(block):
        for q in range(chunks):
            at = slice(q * LANES, (q + 1) * LANES)
            m = m_run[block, at, :].T
            s = s_run[block, at, :].T
            peak = jnp.max(m, axis=0, keepdims=True)
            total = jnp.sum(s * jnp.exp2(m - peak), axis=0, keepdims=True)
            row_part[0, block, row_slot, q : q + 1, :] = peak + jnp.log2(total)
        send_row_sums(0, block)

    def multiply(now, stage):
        i, at = now
        products(i, (at, at + 1), stage)

    def fold_in(now, stage, terms):
        i, at = now
        update(i, (at, at + 1), stage, terms)

    def terms_of(now):
        i, at = now
        bias = bias_of(i, at)
        return [column_term(k) + bias for k in (at, at + 1)]

    now = step_at(0)
    receive_theirs(0)
    multiply(now, stage_a)
    fold_in(now, stage_a, terms_of(now))
    receive(1)
    wait_rows(0)
    pass_rows(1)
    pass_rows(3)
    receive_theirs(1)
    multiply(step_at(1), stage_a)

    def turn(j, carry):
        @pl.when(j == 6)
        def _():
            fold_log_rows(0)

        now, later, last = carry

        @pl.when(j == 0)
        def _():
            receive(2)
            receive(3)
            receive_theirs(2)

        @pl.when(j == 1)
        def _():
            receive(4)
            receive_theirs(4)

        @pl.when(j == 2)
        def _():
            receive(5)

        @pl.when(j == 3)
        def _():
            receive(7)

        @pl.when(j == 4)
        def _():
            receive_theirs(5)

        @pl.when(j == 5)
        def _():
            receive_theirs(7)

        terms = terms_of(now)
        multiply(later, stage_b)
        fold_in(now, stage_a, terms)

        @pl.when(j == 0)
        def _():
            receive_theirs(3)

        @pl.when(j == 1)
        def _():
            for i in (2, 1, 3):
                wait_rows(i)

        @pl.when(j == 2)
        def _():
            receive(6)

        @pl.when(j == 4)
        def _():
            receive_theirs(6)

        terms = terms_of(later)
        multiply(last, stage_a)
        fold_in(later, stage_b, terms)
        return last, step_at(2 * j + 4), step_at(2 * j + 5)

    now, _, _ = lax.fori_loop(0, 7, turn, (step_at(1), step_at(2), step_at(3)))
    fold_in(now, stage_a, terms_of(now))
    fold_log_rows(1)
    logw_copy.wait()

    def finish_log_rows(block):
        parts = take_row_sums(0, block)
        peak = functools.reduce(jnp.maximum, parts)
        total = sum(jnp.exp2(v - peak) for v in parts)
        b = LOG2E * row_logw[block] - (peak + jnp.log2(total))
        b_keep[block] = b
        spread_rows(block, b)

    groups = LANES // 8

    def tree(op, v):
        while v.shape[0] > 1:
            n = v.shape[0] // 2
            v = op(v[:n], v[n:])
        return v[0]

    def lane_tiles(v):
        return [v[..., i * LANES : (i + 1) * LANES] for i in range(halves)]

    def tiles_of(pair):
        return [(k, slice(i * LANES, (i + 1) * LANES)) for k in pair for i in range(halves)]

    def log_columns(pair, block):
        tiles = tiles_of(pair)
        biases = [bias_of(block, k) for k in pair]
        peaks = [jnp.full((8, LANES), NEG, jnp.float32)] * len(tiles)
        totals = [jnp.zeros((8, LANES), jnp.float32)] * len(tiles)
        for q in range(chunks):
            at = slice(q * LANES, (q + 1) * LANES)
            row_term = b_col[block, at, :]
            for n, (k, lanes) in enumerate(tiles):
                t = prod[k, block, at, lanes] + row_term
                prod[k, block, at, lanes] = t
                t = t.reshape(groups, 8, LANES)
                new = jnp.maximum(peaks[n], tree(jnp.maximum, t))
                totals[n] = totals[n] * jnp.exp2(peaks[n] - new) + tree(
                    jnp.add, jnp.exp2(t - new[None])
                )
                peaks[n] = new
        parts = []
        for n in range(len(tiles)):
            top = jnp.max(peaks[n], axis=0, keepdims=True)
            total = jnp.sum(totals[n] * jnp.exp2(peaks[n] - top), axis=0, keepdims=True)
            parts.append(top + jnp.log2(total) + biases[n // halves])
        return parts

    def log_first(pair):
        for (k, lanes), part in zip(tiles_of(pair), log_columns(pair, 0)):
            col_part[0, k, :, lanes] = part

    def log_second(pair):
        for (k, lanes), two in zip(tiles_of(pair), log_columns(pair, 1)):
            one = col_part[0, k, :, lanes]
            top = jnp.maximum(one, two)
            col_part[0, k, :, lanes] = top + jnp.log2(jnp.exp2(one - top) + jnp.exp2(two - top))

    def sum_columns(pair, block):
        tiles = tiles_of(pair)

        def some(q, carry):
            at = pl.ds(pl.multiple_of(q * LANES, LANES), LANES)
            row_term = b_col[block, at, :]
            out = []
            for (k, lanes), total in zip(tiles, carry):
                t = (prod[k, block, at, lanes] * row_term).reshape(4, 4, 8, LANES)
                out.append(total + ((t[0] + t[1]) + (t[2] + t[3])))
            return tuple(out)

        start = (jnp.zeros((4, 8, LANES), jnp.float32),) * len(tiles)
        totals = lax.fori_loop(0, chunks, some, start, unroll=4)
        return [jnp.sum(tree(jnp.add, total), axis=0, keepdims=True) for total in totals]

    def sum_first(pair):
        for (k, lanes), part in zip(tiles_of(pair), sum_columns(pair, 0)):
            col_part[1, k, :, lanes] = part

    def sum_second(pair):
        for (k, lanes), part in zip(tiles_of(pair), sum_columns(pair, 1)):
            col_part[1, k, :, lanes] = col_part[1, k, :, lanes] + part

    def all_chips(visit):
        def one(n, carry):
            visit((2 * n, 2 * n + 1))
            return carry

        lax.fori_loop(0, GROUP // 2, one, 0)

    def column_pass(visit):
        def start(message, k):
            pltpu.make_async_remote_copy(
                src_ref=col_part.at[1, k],
                dst_ref=col_in.at[message],
                send_sem=col_send.at[0],
                recv_sem=col_recv.at[0],
                device_id={"tile": base + k},
                device_id_type=MESH,
            ).start()

        def both(step, at):
            visit((at, at + 1))
            start(2 * step, at + core)
            start(2 * step + 1, at + 1 - core)

        each_chip(both)
        visit((slot - core, slot - core + 1))
        start(GROUP - 2, partner_slot)
        col_in[GROUP - 1] = col_part[1, slot]
        view = col_in.at[pl.ds(0, GROUP - 1)]
        pltpu.make_async_copy(view, view, col_recv.at[0]).wait()
        return col_in[...]

    finish_log_rows(0)
    all_chips(log_first)
    finish_log_rows(1)
    groups_of_chips = ((0, 4), (4, 6), (6, 8))

    def share_columns(g):
        begin, end = groups_of_chips[g]
        these = pl.ds(2 * begin, 2 * (end - begin))
        col_all[slot, these] = col_part[0, these]

        def start(message, to):
            pltpu.make_async_remote_copy(
                src_ref=col_part.at[0, these],
                dst_ref=col_all.at[slot, these],
                send_sem=all_send.at[g],
                recv_sem=all_recv.at[g],
                device_id={"tile": base + to},
                device_id_type=MESH,
            ).start()

        to_others(start)

    def wait_columns(g, sem):
        begin, end = groups_of_chips[g]
        view = col_all.at[pl.ds(0, GROUP - 1), pl.ds(2 * begin, 2 * (end - begin))]
        pltpu.make_async_copy(view, view, sem).wait()

    def take_columns(g):
        wait_columns(g, all_recv.at[g])
        begin, end = groups_of_chips[g]
        for k in range(2 * begin, 2 * end):
            parts = [col_all[i, k] for i in range(GROUP)]
            peak = functools.reduce(jnp.maximum, parts)
            total = sum(jnp.exp2(v - peak) for v in parts)
            weights = tgt[k, shard:].astype(jnp.float32)
            weights = weights[3:4] + weights[4:5] + weights[5:6]
            a = LOG2E * weights - (peak + jnp.log2(total))
            a_all[k] = a
            for i in range(2):
                a_wide[i, k] = jnp.broadcast_to(a + bias_of(i, k), (8, shard))

    for g, (begin, end) in enumerate(groups_of_chips):

        def one(n, carry):
            log_second((2 * n, 2 * n + 1))
            return carry

        lax.fori_loop(begin, end, one, 0)
        share_columns(g)

    step_rows = 128

    def plan_rows(block, chips, more):
        slots = range(2 * chips[0], 2 * chips[1])

        def some(step, carry):
            at = pl.ds(pl.multiple_of(step * step_rows, step_rows), step_rows)
            totals = [jnp.zeros((step_rows // 8, 8, LANES), jnp.float32)] * 2
            if more:
                totals[0] = s_run[block, at, :].reshape(step_rows // 8, 8, LANES)
            for n, k in enumerate(slots):
                t = jnp.exp2(
                    prod[k, block, at, :].reshape(step_rows // 8, 8, shard)
                    + a_wide[block, k][None]
                )
                prod[k, block, at, :] = t.reshape(step_rows, shard)
                totals[n % 2] = totals[n % 2] + sum(lane_tiles(t))
            s_run[block, at, :] = sum(totals).reshape(step_rows, LANES)
            return carry

        lax.fori_loop(0, rows // step_rows, some, 0)

    def fold_rows(block):
        for q in range(chunks):
            at = slice(q * LANES, (q + 1) * LANES)
            row_part[1, block, row_slot, q : q + 1, :] = jnp.sum(
                s_run[block, at, :].T, axis=0, keepdims=True
            )
        send_row_sums(1, block)

    def finish_rows(block):
        total = sum(take_row_sums(1, block))
        spread_rows(block, jnp.exp2(LOG2E * row_logw[block]) / total)
        b_keep[block] = b_keep[block] + LOG2E * row_logw[block] - jnp.log2(total)

    take_columns(0)
    plan_rows(0, (0, 4), False)
    take_columns(1)
    plan_rows(0, (4, 6), True)
    plan_rows(1, (0, 4), False)
    take_columns(2)
    plan_rows(0, (6, 8), True)
    fold_rows(0)
    plan_rows(1, (4, 8), True)
    fold_rows(1)
    finish_rows(0)
    all_chips(sum_first)

    view = tgt.at[pl.ds(0, GROUP - 1)]
    pltpu.make_async_copy(view, view, gather_send.at[0]).wait()
    view = src.at[0, pl.ds(0, 3 * quarter)]
    pltpu.make_async_copy(view, view, src_send.at[1]).wait()
    for g in range(len(groups_of_chips)):
        wait_columns(g, all_send.at[g])

    finish_rows(1)

    total = jnp.sum(column_pass(sum_second), axis=0)
    a = a_all[slot] + LOG2E * col_logw[...] - jnp.log2(total)

    row_out[...] = row_sq[...] / depth + dual_scale * b_keep[half]
    col_out[...] = own_sq / depth + dual_scale * a

    for iteration in range(2):
        for block in range(2):
            view = row_part.at[iteration, block, pl.ds(0, len(row_peers))]
            pltpu.make_async_copy(view, view, row_send.at[iteration, block]).wait()
    view = col_in.at[pl.ds(0, GROUP - 1)]
    pltpu.make_async_copy(view, view, col_send.at[0]).wait()


def per_device(source, target, row_logw, col_logw, support):
    rows, depth = source.shape
    shard = target.shape[0]
    vmem = pl.BlockSpec(memory_space=pltpu.VMEM)
    f32 = jnp.float32
    row_dual, col_dual = pl.pallas_call(
        kernel,
        out_shape=(
            jax.ShapeDtypeStruct((rows // LANES, LANES), f32),
            jax.ShapeDtypeStruct((1, shard), f32),
        ),
        in_specs=[pl.BlockSpec(memory_space=pl.ANY)] * 5,
        out_specs=(vmem, vmem),
        scratch_shapes=[
            pltpu.VMEM((2, rows, depth), source.dtype),
            pltpu.VMEM((GROUP, shard + 16, depth), target.dtype),
            pltpu.VMEM((2, rows // LANES, LANES), f32),
            pltpu.VMEM((1, shard), f32),
            pltpu.SMEM(support.shape, support.dtype),
            pltpu.VMEM((GROUP, 2, rows, shard), f32),
            pltpu.VMEM((2, rows, shard), f32),
            pltpu.VMEM((2, rows, shard), f32),
            pltpu.VMEM((2, rows, LANES), f32),
            pltpu.VMEM((2, rows, LANES), f32),
            pltpu.VMEM((2, rows, LANES), f32),
            pltpu.VMEM((2, rows // LANES, LANES), f32),
            pltpu.VMEM((GROUP, 1, shard), f32),
            pltpu.VMEM((2, GROUP, 8, shard), f32),
            pltpu.VMEM((rows // LANES, LANES), f32),
            pltpu.VMEM((2, 2, 2 * REPS, rows // LANES, LANES), f32),
            pltpu.VMEM((2, GROUP, 1, shard), f32),
            pltpu.VMEM((GROUP, GROUP, 1, shard), f32),
            pltpu.VMEM((GROUP, 1, shard), f32),
            pltpu.SemaphoreType.DMA((5,)),
            pltpu.SemaphoreType.DMA((2,)),
            pltpu.SemaphoreType.DMA((2,)),
            pltpu.SemaphoreType.DMA((REPS,)),
            pltpu.SemaphoreType.DMA((1,)),
            pltpu.SemaphoreType.DMA((GROUP,)),
            pltpu.SemaphoreType.DMA((3,)),
            pltpu.SemaphoreType.DMA((3,)),
            pltpu.SemaphoreType.DMA((2, 2)),
            pltpu.SemaphoreType.DMA((2, 2)),
            pltpu.SemaphoreType.DMA((1,)),
            pltpu.SemaphoreType.DMA((1,)),
        ],
        compiler_params=pltpu.CompilerParams(
            collective_id=0, has_side_effects=True, vmem_limit_bytes=63 * 1024 * 1024
        ),
        name="sinkhorn",
    )(
        source,
        target,
        row_logw.reshape(rows // LANES, LANES),
        col_logw.reshape(1, shard),
        support,
    )
    return row_dual.reshape(rows), col_dual.reshape(shard)


def solution(mesh):
    placed = (P("tile", None), P(("rep", "tile"), None), P("tile"), P(("rep", "tile")), P())
    return jax.shard_map(
        per_device,
        mesh=mesh,
        in_specs=placed,
        out_specs=(P("tile"), P(("rep", "tile"))),
        check_vma=False,
    )
```

```python
import functools
import math

import jax
import jax.numpy as jnp
from jax import lax
from jax.experimental import pallas as pl
from jax.experimental.pallas import tpu as pltpu
from jax.sharding import PartitionSpec as P

MESH = pl.DeviceIdType.MESH
EPS = 0.1
NEG = -1e30
LOG2E = 1.0 / math.log(2.0)
LN2 = math.log(2.0)
NX = 4
TILES = 2 * NX * NX
GROUP = TILES // 2
REPS = 4
LANES = 128


def kernel(
    source_hbm,
    target_hbm,
    row_logw_hbm,
    col_logw_hbm,
    support_hbm,
    row_out,
    col_out,
    src,
    tgt,
    row_logw,
    col_logw,
    support,
    prod,
    stage_a,
    stage_b,
    m_run,
    s_run,
    b_col,
    b_keep,
    a_all,
    a_wide,
    row_sq,
    row_part,
    col_part,
    col_all,
    col_in,
    local_sem,
    logw_sem,
    src_send,
    src_recv,
    gather_send,
    gather_recv,
    all_send,
    all_recv,
    row_send,
    row_recv,
    col_send,
    col_recv,
):
    rows = src.shape[1]
    shard = col_logw.shape[1]
    depth = src.shape[2]
    blocks = TILES * shard // rows
    per_block = TILES // blocks
    chunks = rows // LANES
    halves = shard // LANES
    me = lax.axis_index("tile")
    rep = lax.axis_index("rep")
    core = me % 2
    x = me // (2 * NX)
    z = (me // 2) % NX
    half = x // 2
    xl = x % 2
    base = half * GROUP
    slot = me - base
    partner = me + 1 - 2 * core
    across = ((NX - 1 - x) * NX + z) * 2 + core
    row_tiles = [me * (1 - half) + across * half, across * (1 - half) + me * half]
    score_scale = 2.0 * LOG2E / (depth * EPS)
    square_scale = LOG2E / (depth * EPS)
    dual_scale = EPS * LN2

    zs = [(z + i) % NX for i in range(NX)]
    xls = [xl, 1 - xl]

    def place(dx, dz, of):
        return (xls[dx] * NX + zs[dz]) * 2 + of

    def mine(dx, dz):
        return place(dx, dz, core)

    def theirs(dx, dz):
        return place(dx, dz, 1 - core)

    def chip(step):
        m = NX - 1 - step % NX
        dz = m + m // 2 - 2 * (m // 3)
        return (((xl + 1 - step // NX) % 2) * NX + (z + dz) % NX) * 2

    def each_chip(visit):
        def one(step, at):
            visit(step, at)
            return chip(step + 1)

        lax.fori_loop(0, GROUP // 2 - 1, one, chip(0))

    def to_others(start):
        def both(step, at):
            start(2 * step, at + core)
            start(2 * step + 1, at + 1 - core)

        each_chip(both)
        start(GROUP - 2, slot + 1 - 2 * core)

    def reached(j, c):
        return (j + 16 - c) // 16

    def pair_at(p):
        turn = (p + 1) % 3
        dz = (1 + 2 * turn - 3 * (turn // 2)) * reached(p, 2)
        dx = reached(p, 1) - reached(p, 2) + reached(p, 5)
        return (((xl + dx) % 2) * NX + (z + dz) % NX) * 2

    row_peers = [{"tile": me, "rep": (rep + i) % REPS} for i in range(1, REPS)]
    row_peers += [{"tile": across, "rep": (rep + i) % REPS} for i in range(REPS)]

    loads = [
        pltpu.make_async_copy(target_hbm, tgt.at[slot, pl.ds(0, shard)], local_sem.at[0]),
        pltpu.make_async_copy(source_hbm, src.at[half], local_sem.at[1]),
        pltpu.make_async_copy(support_hbm, support, local_sem.at[2]),
        pltpu.make_async_copy(row_logw_hbm, row_logw.at[half], local_sem.at[3]),
        pltpu.make_async_copy(col_logw_hbm, col_logw, local_sem.at[4]),
    ]
    for load in loads:
        load.start()

    barrier = pltpu.get_barrier_semaphore()

    def greet(message, at):
        pl.semaphore_signal(
            barrier, inc=1, device_id={"tile": base + at}, device_id_type=MESH
        )

    to_others(greet)
    for peer in row_peers:
        pl.semaphore_signal(barrier, inc=1, device_id=peer, device_id_type=MESH)

    loads[0].wait()
    loads[4].wait()
    own = tgt[slot, :shard].astype(jnp.float32)
    own_sq = jnp.sum((own * own).T, axis=0, keepdims=True)
    parts = []
    for rest in (-square_scale * own_sq, col_logw[...]):
        for _ in range(3):
            parts.append(rest.astype(jnp.bfloat16))
            rest = rest - parts[-1].astype(jnp.float32)
    extra = tgt.shape[1] - shard
    tgt[slot, shard:] = jnp.concatenate(
        parts + [jnp.zeros((extra - 6, depth), jnp.bfloat16)], axis=0
    )

    pl.semaphore_wait(barrier, GROUP - 1 + len(row_peers))

    quarter = rows // REPS

    def rows_at(i):
        return pl.ds(pl.multiple_of((rep + i) % REPS * quarter, quarter), quarter)

    def send_rows(i, sem):
        pltpu.make_async_remote_copy(
            src_ref=source_hbm.at[rows_at(i)],
            dst_ref=src.at[half, rows_at(i)],
            send_sem=src_send.at[sem],
            recv_sem=src_recv.at[(rep + i) % REPS],
            device_id={"tile": across},
            device_id_type=MESH,
        ).start()

    def wait_rows(i):
        view = src.at[1 - half, rows_at(i)]
        pltpu.make_async_copy(view, view, src_recv.at[(rep + i) % REPS]).wait()

    def pass_rows(to):
        view = src.at[1 - half, rows_at(0)]
        pltpu.make_async_remote_copy(
            src_ref=view,
            dst_ref=view,
            send_sem=src_send.at[1],
            recv_sem=src_recv.at[rep],
            device_id={"rep": (rep + to) % REPS},
            device_id_type=MESH,
        ).start()

    def send_shard(k, to):
        pltpu.make_async_remote_copy(
            src_ref=tgt.at[k],
            dst_ref=tgt.at[k],
            send_sem=gather_send.at[0],
            recv_sem=gather_recv.at[k],
            device_id={"tile": base + to},
            device_id_type=MESH,
        ).start()

    def wait_shard(k):
        pltpu.make_async_copy(tgt.at[k], tgt.at[k], gather_recv.at[k]).wait()

    partner_slot = slot + 1 - 2 * core
    send_rows(0, 0)
    send_shard(slot, mine(1, 0))
    for dz in (1, 3):
        send_shard(slot, mine(0, dz))
    send_shard(slot, partner_slot)
    logw_copy = pltpu.make_async_remote_copy(
        src_ref=row_logw_hbm,
        dst_ref=row_logw.at[half],
        send_sem=logw_sem.at[0],
        recv_sem=logw_sem.at[1],
        device_id={"tile": across},
        device_id_type=MESH,
    )
    logw_copy.start()

    def bias_of(i, k):
        tile = row_tiles[0] * (1 - i) + row_tiles[1] * i
        live = support[tile, rep * blocks + (base + k) // per_block]
        return (1.0 - live.astype(jnp.float32)) * NEG

    for load in loads[1:4]:
        load.wait()

    m_run[...] = jnp.full(m_run.shape, NEG, jnp.float32)
    s_run[...] = jnp.zeros(s_run.shape, jnp.float32)
    for q in range(chunks):
        cells = src[half, q * LANES : (q + 1) * LANES, :].astype(jnp.float32)
        sq = cells * cells
        sq = sum(sq[:, i * LANES : (i + 1) * LANES] for i in range(depth // LANES))
        row_sq[q : q + 1, :] = jnp.sum(sq.T, axis=0, keepdims=True)

    view = src.at[0, pl.ds(0, quarter)]
    pltpu.make_async_copy(view, view, src_send.at[0]).wait()
    send_rows(2, 1)
    send_shard(slot, mine(0, 2))

    def against(left, right):
        return lax.dot_general(
            left, right, (((1,), (1,)), ((), ())), preferred_element_type=jnp.float32
        )

    def products(i, pair, stage):
        for n, k in enumerate(pair):
            for r in range(0, rows, 512):
                stage[n, r : r + 512, :] = against(src[i, r : r + 512, :], tgt[k, :shard])

    def column_term(k):
        parts = tgt[k, shard:].astype(jnp.float32)
        return parts[0:1] + parts[1:2] + parts[2:3]

    def update(i, pair, stage, terms):
        step = 32
        for r in range(0, rows, step):
            at = slice(r, r + step)
            t = []
            for n, k in enumerate(pair):
                p = stage[n, at, :] * score_scale
                prod[k, i, at, :] = p
                t.extend(
                    p[:, h * LANES : (h + 1) * LANES] + terms[n][:, h * LANES : (h + 1) * LANES]
                    for h in range(halves)
                )
            old = m_run[i, at, :]
            new = functools.reduce(jnp.maximum, t, old)
            m_run[i, at, :] = new
            s_run[i, at, :] = s_run[i, at, :] * jnp.exp2(old - new) + sum(
                jnp.exp2(v - new) for v in t
            )

    def receive(p):
        k = pair_at(p) + core
        wait_shard(k)
        send_shard(k, partner_slot)

        @pl.when(core * 8 + p == 1)
        def _():
            for dz in (1, 3, 2):
                send_shard(k, mine(0, dz))

        @pl.when(core * reached(p, 2) * (1 - reached(p, 5)) == 1)
        def _():
            send_shard(k, mine(1, 0))

    def receive_theirs(p):
        wait_shard(pair_at(p) + 1 - core)

    def rows_of(other):
        return half + other * (1 - 2 * half)

    def step_at(n):
        a, b, c = reached(n, 5), reached(n, 10), reached(n, 13)
        at = pair_at(n - 5 * a - 3 * c)
        return half * (1 - a) + (1 - half) * (a - b) + c, at

    row_slot = half * REPS + rep

    def send_row_sums(iteration, block):
        for peer in row_peers:
            pltpu.make_async_remote_copy(
                src_ref=row_part.at[iteration, block, row_slot],
                dst_ref=row_part.at[iteration, block, row_slot],
                send_sem=row_send.at[iteration, block],
                recv_sem=row_recv.at[iteration, block],
                device_id=peer,
                device_id_type=MESH,
            ).start()

    def take_row_sums(iteration, block):
        view = row_part.at[iteration, block, pl.ds(0, len(row_peers))]
        pltpu.make_async_copy(view, view, row_recv.at[iteration, block]).wait()
        return [row_part[iteration, block, i] for i in range(2 * REPS)]

    def spread_rows(block, values):
        for q in range(chunks):
            b_col[block, q * LANES : (q + 1) * LANES, :] = jnp.broadcast_to(
                values[q : q + 1, :], (LANES, LANES)
            ).T

    def fold_log_rows(block):
        for q in range(chunks):
            at = slice(q * LANES, (q + 1) * LANES)
            m = m_run[block, at, :].T
            s = s_run[block, at, :].T
            peak = jnp.max(m, axis=0, keepdims=True)
            total = jnp.sum(s * jnp.exp2(m - peak), axis=0, keepdims=True)
            row_part[0, block, row_slot, q : q + 1, :] = peak + jnp.log2(total)
        send_row_sums(0, block)

    def multiply(now, stage):
        i, at = now
        products(i, (at, at + 1), stage)

    def fold_in(now, stage, terms):
        i, at = now
        update(i, (at, at + 1), stage, terms)

    def terms_of(now):
        i, at = now
        bias = bias_of(i, at)
        return [column_term(k) + bias for k in (at, at + 1)]

    now = step_at(0)
    receive_theirs(0)
    multiply(now, stage_a)
    fold_in(now, stage_a, terms_of(now))
    receive(1)
    wait_rows(0)
    pass_rows(1)
    pass_rows(3)
    receive_theirs(1)
    multiply(step_at(1), stage_a)

    def turn(j, carry):
        @pl.when(j == 6)
        def _():
            fold_log_rows(0)

        now, later, last = carry

        @pl.when(j == 0)
        def _():
            receive(2)
            receive(3)
            receive_theirs(2)

        @pl.when(j == 1)
        def _():
            receive(4)
            receive_theirs(4)

        @pl.when(j == 2)
        def _():
            receive(5)

        @pl.when(j == 3)
        def _():
            receive(7)

        @pl.when(j == 4)
        def _():
            receive_theirs(5)

        @pl.when(j == 5)
        def _():
            receive_theirs(7)

        terms = terms_of(now)
        multiply(later, stage_b)
        fold_in(now, stage_a, terms)

        @pl.when(j == 0)
        def _():
            receive_theirs(3)

        @pl.when(j == 1)
        def _():
            for i in (2, 1, 3):
                wait_rows(i)

        @pl.when(j == 2)
        def _():
            receive(6)

        @pl.when(j == 4)
        def _():
            receive_theirs(6)

        terms = terms_of(later)
        multiply(last, stage_a)
        fold_in(later, stage_b, terms)
        return last, step_at(2 * j + 4), step_at(2 * j + 5)

    now, _, _ = lax.fori_loop(0, 7, turn, (step_at(1), step_at(2), step_at(3)))
    fold_in(now, stage_a, terms_of(now))
    fold_log_rows(1)
    logw_copy.wait()

    def finish_log_rows(block):
        parts = take_row_sums(0, block)
        peak = functools.reduce(jnp.maximum, parts)
        total = sum(jnp.exp2(v - peak) for v in parts)
        b = LOG2E * row_logw[block] - (peak + jnp.log2(total))
        b_keep[block] = b
        spread_rows(block, b)

    groups = LANES // 8

    def tree(op, v):
        while v.shape[0] > 1:
            n = v.shape[0] // 2
            v = op(v[:n], v[n:])
        return v[0]

    def lane_tiles(v):
        return [v[..., i * LANES : (i + 1) * LANES] for i in range(halves)]

    def tiles_of(pair):
        return [(k, slice(i * LANES, (i + 1) * LANES)) for k in pair for i in range(halves)]

    def log_columns(pair, block):
        tiles = tiles_of(pair)
        biases = [bias_of(block, k) for k in pair]
        peaks = [jnp.full((8, LANES), NEG, jnp.float32)] * len(tiles)
        totals = [jnp.zeros((8, LANES), jnp.float32)] * len(tiles)
        for q in range(chunks):
            at = slice(q * LANES, (q + 1) * LANES)
            row_term = b_col[block, at, :]
            for n, (k, lanes) in enumerate(tiles):
                t = prod[k, block, at, lanes] + row_term
                prod[k, block, at, lanes] = t
                t = t.reshape(groups, 8, LANES)
                new = jnp.maximum(peaks[n], tree(jnp.maximum, t))
                totals[n] = totals[n] * jnp.exp2(peaks[n] - new) + tree(
                    jnp.add, jnp.exp2(t - new[None])
                )
                peaks[n] = new
        parts = []
        for n in range(len(tiles)):
            top = jnp.max(peaks[n], axis=0, keepdims=True)
            total = jnp.sum(totals[n] * jnp.exp2(peaks[n] - top), axis=0, keepdims=True)
            parts.append(top + jnp.log2(total) + biases[n // halves])
        return parts

    def log_first(pair):
        for (k, lanes), part in zip(tiles_of(pair), log_columns(pair, 0)):
            col_part[0, k, :, lanes] = part

    def log_second(pair):
        for (k, lanes), two in zip(tiles_of(pair), log_columns(pair, 1)):
            one = col_part[0, k, :, lanes]
            top = jnp.maximum(one, two)
            col_part[0, k, :, lanes] = top + jnp.log2(jnp.exp2(one - top) + jnp.exp2(two - top))

    def sum_columns(pair, block):
        tiles = tiles_of(pair)

        def some(q, carry):
            at = pl.ds(pl.multiple_of(q * LANES, LANES), LANES)
            row_term = b_col[block, at, :]
            out = []
            for (k, lanes), total in zip(tiles, carry):
                t = (prod[k, block, at, lanes] * row_term).reshape(4, 4, 8, LANES)
                out.append(total + ((t[0] + t[1]) + (t[2] + t[3])))
            return tuple(out)

        start = (jnp.zeros((4, 8, LANES), jnp.float32),) * len(tiles)
        totals = lax.fori_loop(0, chunks, some, start, unroll=4)
        return [jnp.sum(tree(jnp.add, total), axis=0, keepdims=True) for total in totals]

    def sum_first(pair):
        for (k, lanes), part in zip(tiles_of(pair), sum_columns(pair, 0)):
            col_part[1, k, :, lanes] = part

    def sum_second(pair):
        for (k, lanes), part in zip(tiles_of(pair), sum_columns(pair, 1)):
            col_part[1, k, :, lanes] = col_part[1, k, :, lanes] + part

    def all_chips(visit):
        def one(n, carry):
            visit((2 * n, 2 * n + 1))
            return carry

        lax.fori_loop(0, GROUP // 2, one, 0)

    def column_pass(visit):
        def start(message, k):
            pltpu.make_async_remote_copy(
                src_ref=col_part.at[1, k],
                dst_ref=col_in.at[message],
                send_sem=col_send.at[0],
                recv_sem=col_recv.at[0],
                device_id={"tile": base + k},
                device_id_type=MESH,
            ).start()

        def both(step, at):
            visit((at, at + 1))
            start(2 * step, at + core)
            start(2 * step + 1, at + 1 - core)

        each_chip(both)
        visit((slot - core, slot - core + 1))
        start(GROUP - 2, partner_slot)
        col_in[GROUP - 1] = col_part[1, slot]
        view = col_in.at[pl.ds(0, GROUP - 1)]
        pltpu.make_async_copy(view, view, col_recv.at[0]).wait()
        return col_in[...]

    finish_log_rows(0)
    all_chips(log_first)
    finish_log_rows(1)
    groups_of_chips = ((0, 4), (4, 6), (6, 8))

    def share_columns(g):
        begin, end = groups_of_chips[g]
        these = pl.ds(2 * begin, 2 * (end - begin))
        col_all[slot, these] = col_part[0, these]

        def start(message, to):
            pltpu.make_async_remote_copy(
                src_ref=col_part.at[0, these],
                dst_ref=col_all.at[slot, these],
                send_sem=all_send.at[g],
                recv_sem=all_recv.at[g],
                device_id={"tile": base + to},
                device_id_type=MESH,
            ).start()

        to_others(start)

    def wait_columns(g, sem):
        begin, end = groups_of_chips[g]
        view = col_all.at[pl.ds(0, GROUP - 1), pl.ds(2 * begin, 2 * (end - begin))]
        pltpu.make_async_copy(view, view, sem).wait()

    def take_columns(g):
        wait_columns(g, all_recv.at[g])
        begin, end = groups_of_chips[g]
        for k in range(2 * begin, 2 * end):
            parts = [col_all[i, k] for i in range(GROUP)]
            peak = functools.reduce(jnp.maximum, parts)
            total = sum(jnp.exp2(v - peak) for v in parts)
            weights = tgt[k, shard:].astype(jnp.float32)
            weights = weights[3:4] + weights[4:5] + weights[5:6]
            a = LOG2E * weights - (peak + jnp.log2(total))
            a_all[k] = a
            for i in range(2):
                a_wide[i, k] = jnp.broadcast_to(a + bias_of(i, k), (8, shard))

    for g, (begin, end) in enumerate(groups_of_chips):

        def one(n, carry):
            log_second((2 * n, 2 * n + 1))
            return carry

        lax.fori_loop(begin, end, one, 0)
        share_columns(g)

    step_rows = 256

    def plan_rows(block, chips, more):
        slots = range(2 * chips[0], 2 * chips[1])

        def some(step, carry):
            at = pl.ds(pl.multiple_of(step * step_rows, step_rows), step_rows)
            totals = [jnp.zeros((step_rows // 8, 8, LANES), jnp.float32)] * 2
            if more:
                totals[0] = s_run[block, at, :].reshape(step_rows // 8, 8, LANES)
            for n, k in enumerate(slots):
                t = jnp.exp2(
                    prod[k, block, at, :].reshape(step_rows // 8, 8, shard)
                    + a_wide[block, k][None]
                )
                prod[k, block, at, :] = t.reshape(step_rows, shard)
                totals[n % 2] = totals[n % 2] + sum(lane_tiles(t))
            s_run[block, at, :] = sum(totals).reshape(step_rows, LANES)
            return carry

        lax.fori_loop(0, rows // step_rows, some, 0)

    def fold_rows(block):
        for q in range(chunks):
            at = slice(q * LANES, (q + 1) * LANES)
            row_part[1, block, row_slot, q : q + 1, :] = jnp.sum(
                s_run[block, at, :].T, axis=0, keepdims=True
            )
        send_row_sums(1, block)

    def finish_rows(block):
        total = sum(take_row_sums(1, block))
        spread_rows(block, jnp.exp2(LOG2E * row_logw[block]) / total)
        b_keep[block] = b_keep[block] + LOG2E * row_logw[block] - jnp.log2(total)

    take_columns(0)
    plan_rows(0, (0, 4), False)
    take_columns(1)
    plan_rows(0, (4, 6), True)
    plan_rows(1, (0, 4), False)
    take_columns(2)
    plan_rows(0, (6, 8), True)
    fold_rows(0)
    plan_rows(1, (4, 8), True)
    fold_rows(1)
    finish_rows(0)
    all_chips(sum_first)

    view = tgt.at[pl.ds(0, GROUP - 1)]
    pltpu.make_async_copy(view, view, gather_send.at[0]).wait()
    view = src.at[0, pl.ds(0, 3 * quarter)]
    pltpu.make_async_copy(view, view, src_send.at[1]).wait()
    for g in range(len(groups_of_chips)):
        wait_columns(g, all_send.at[g])

    finish_rows(1)

    total = jnp.sum(column_pass(sum_second), axis=0)
    a = a_all[slot] + LOG2E * col_logw[...] - jnp.log2(total)

    row_out[...] = row_sq[...] / depth + dual_scale * b_keep[half]
    col_out[...] = own_sq / depth + dual_scale * a

    for iteration in range(2):
        for block in range(2):
            view = row_part.at[iteration, block, pl.ds(0, len(row_peers))]
            pltpu.make_async_copy(view, view, row_send.at[iteration, block]).wait()
    view = col_in.at[pl.ds(0, GROUP - 1)]
    pltpu.make_async_copy(view, view, col_send.at[0]).wait()


def per_device(source, target, row_logw, col_logw, support):
    rows, depth = source.shape
    shard = target.shape[0]
    vmem = pl.BlockSpec(memory_space=pltpu.VMEM)
    f32 = jnp.float32
    row_dual, col_dual = pl.pallas_call(
        kernel,
        out_shape=(
            jax.ShapeDtypeStruct((rows // LANES, LANES), f32),
            jax.ShapeDtypeStruct((1, shard), f32),
        ),
        in_specs=[pl.BlockSpec(memory_space=pl.ANY)] * 5,
        out_specs=(vmem, vmem),
        scratch_shapes=[
            pltpu.VMEM((2, rows, depth), source.dtype),
            pltpu.VMEM((GROUP, shard + 16, depth), target.dtype),
            pltpu.VMEM((2, rows // LANES, LANES), f32),
            pltpu.VMEM((1, shard), f32),
            pltpu.SMEM(support.shape, support.dtype),
            pltpu.VMEM((GROUP, 2, rows, shard), f32),
            pltpu.VMEM((2, rows, shard), f32),
            pltpu.VMEM((2, rows, shard), f32),
            pltpu.VMEM((2, rows, LANES), f32),
            pltpu.VMEM((2, rows, LANES), f32),
            pltpu.VMEM((2, rows, LANES), f32),
            pltpu.VMEM((2, rows // LANES, LANES), f32),
            pltpu.VMEM((GROUP, 1, shard), f32),
            pltpu.VMEM((2, GROUP, 8, shard), f32),
            pltpu.VMEM((rows // LANES, LANES), f32),
            pltpu.VMEM((2, 2, 2 * REPS, rows // LANES, LANES), f32),
            pltpu.VMEM((2, GROUP, 1, shard), f32),
            pltpu.VMEM((GROUP, GROUP, 1, shard), f32),
            pltpu.VMEM((GROUP, 1, shard), f32),
            pltpu.SemaphoreType.DMA((5,)),
            pltpu.SemaphoreType.DMA((2,)),
            pltpu.SemaphoreType.DMA((2,)),
            pltpu.SemaphoreType.DMA((REPS,)),
            pltpu.SemaphoreType.DMA((1,)),
            pltpu.SemaphoreType.DMA((GROUP,)),
            pltpu.SemaphoreType.DMA((3,)),
            pltpu.SemaphoreType.DMA((3,)),
            pltpu.SemaphoreType.DMA((2, 2)),
            pltpu.SemaphoreType.DMA((2, 2)),
            pltpu.SemaphoreType.DMA((1,)),
            pltpu.SemaphoreType.DMA((1,)),
        ],
        compiler_params=pltpu.CompilerParams(
            collective_id=0, has_side_effects=True, vmem_limit_bytes=63 * 1024 * 1024
        ),
        name="sinkhorn",
    )(
        source,
        target,
        row_logw.reshape(rows // LANES, LANES),
        col_logw.reshape(1, shard),
        support,
    )
    return row_dual.reshape(rows), col_dual.reshape(shard)


def solution(mesh):
    placed = (P("tile", None), P(("rep", "tile"), None), P("tile"), P(("rep", "tile")), P())
    return jax.shard_map(
        per_device,
        mesh=mesh,
        in_specs=placed,
        out_specs=(P("tile"), P(("rep", "tile"))),
        check_vma=False,
    )
```
